128 devices in a mesh: group: 4 (over z), dev: 32 (over x, y, core).
Axes of the slice: x: 4, y: 4, z: 4, core: 2. Of those that a mesh axis runs over, the one named last changes fastest.
Arguments:
- blocks_in: float32 [3968, 8, 4096], P(('group', 'dev')), as said below
- counts: int32 [128], P(('group', 'dev')), may hold values from 1 to 31, as said below
Outputs:
- blocks_out: float32 [2048, 8, 4096], P(('group', 'dev'))
The draws below stay inside these ranges and needn't reach their ends.
Inputs may be any that keep to these rules, and one draw needn't show every extreme that they name: `blocks_in`: every slot holds a state of positive density and pressure. Device i (in the order of group+dev) holds its live meshblocks in its first counts[i] slots, in curve order. The counts sum to 2048; for every device i, starts[i] - i * 16 lies in 0 .. 15.
All inputs are finite; a program needn't handle non-finite values.
Results may differ from the reference program's by a relative error of at most 0.0003.
Values sent between devices are 32-bit elements; how exact they have to be, the bound alone decides.
No kernel may reach another device: no remote copies, remote signals or barrier semaphores. Data moves between devices by JAX's collectives and lax.ppermute only.
A program may use at most 192 MiB of HBM per device.

```python
import math
import jax
import jax.numpy as jnp
from jax import lax

BS = 16
BRICK_Y = 2
BRICK_Z = 8
BRICK_X = 1
BLK_DEV = 16
FIELDS = 8
DEVS = 128
CAP = 31
BLOCKS = 2048
N_GROUP = 4
N_DEV = 32


GAMMA = 5.0 / 3.0


def draw_counts(key, part):
    key = jax.random.fold_in(key, 1)
    key_offsets, key_place = jax.random.split(key)
    surplus = jax.random.randint(key_offsets, (DEVS + 1,), 0, BLK_DEV).astype(jnp.int32)
    surplus = surplus.at[0].set(0).at[DEVS].set(0)
    chosen = jax.random.randint(key_place, (), 0, DEVS - 2).astype(jnp.int32)
    surplus = surplus.at[chosen].set(0).at[chosen + 1].set(BLK_DEV - 1)
    surplus = surplus.at[DEVS - 1].set(BLK_DEV - 1)
    return (BLK_DEV + surplus[1:] - surplus[:-1]).astype(jnp.int32)


def draw_blocks_in(key, part):
    key = jax.random.fold_in(key, 2)
    keys = jax.random.split(key, 6)
    slots = DEVS * CAP
    cells = BS * BS * BS
    amplitude = jnp.exp(jax.random.uniform(keys[0], (slots, 1, 1), jnp.float32, math.log(0.3), math.log(3.0)))
    motion = jnp.clip(jax.random.normal(keys[1], (slots, 3, cells), jnp.float32), -3.0, 3.0)
    field_noise = jnp.clip(jax.random.normal(keys[2], (slots, 3, cells), jnp.float32), -3.0, 3.0)
    velocity = 0.4 * amplitude * motion
    magnetic = 0.4 * amplitude * field_noise
    density = jax.random.uniform(keys[3], (slots, 1, cells), jnp.float32, 0.5, 1.5)
    pressure = jax.random.uniform(keys[4], (slots, 1, cells), jnp.float32, 0.6, 1.4)
    energy = pressure / (GAMMA - 1.0) + 0.5 * density * jnp.sum(velocity * velocity, axis=1, keepdims=True) + 0.5 * jnp.sum(magnetic * magnetic, axis=1, keepdims=True)
    return jnp.concatenate([density, density * velocity, energy, magnetic], axis=1).astype(jnp.float32)


def setup_inputs(seed: int = 0) -> dict:
    splits = jax.random.split(jax.random.key(seed), 3)
    blocks_in = draw_blocks_in(jax.random.fold_in(splits[2], 71), 0)
    counts = draw_counts(jax.random.fold_in(splits[2], 71), 0)
    return {"blocks_in": blocks_in, "counts": counts}


GAMMA = 5.0 / 3.0
COURANT = 0.25
DENSITY_FLOOR = 0.05
PRESSURE_FLOOR = 0.05

def trimmed(values, along, front, back):
    return lax.slice_in_dim(values, front, values.shape[along] - back, axis=along)

def primitive(state):
    density = jnp.maximum(state[0], DENSITY_FLOOR)
    velocity = state[1:4] / density
    magnetic = state[5:8]
    kinetic = 0.5 * density * lax.optimization_barrier(jnp.sum(velocity * velocity, axis=0))
    magnetic_energy = 0.5 * lax.optimization_barrier(jnp.sum(magnetic * magnetic, axis=0))
    pressure = jnp.maximum((GAMMA - 1.0) * (state[4] - kinetic - magnetic_energy), PRESSURE_FLOOR)
    return jnp.concatenate([density[None], velocity, pressure[None], magnetic], axis=0)

def conserved(prims):
    density = prims[0]
    velocity = prims[1:4]
    magnetic = prims[5:8]
    energy = prims[4] / (GAMMA - 1.0) + 0.5 * density * lax.optimization_barrier(jnp.sum(velocity * velocity, axis=0)) + 0.5 * lax.optimization_barrier(jnp.sum(magnetic * magnetic, axis=0))
    return jnp.concatenate([density[None], density * velocity, energy[None], magnetic], axis=0)

def fast_speed(prims, normal):
    density = prims[0]
    sound = GAMMA * prims[4] / density
    alfven = lax.optimization_barrier(jnp.sum(prims[5:8] * prims[5:8], axis=0)) / density
    along_field = prims[5 + normal] * prims[5 + normal] / density
    total = sound + alfven
    root = jnp.sqrt(jnp.maximum(total * total - 4.0 * sound * along_field, 0.0))
    return jnp.sqrt(0.5 * (total + root))

def physical_flux(prims, state, normal):
    density = prims[0]
    velocity = prims[1:4]
    magnetic = prims[5:8]
    speed_normal = velocity[normal]
    field_normal = magnetic[normal]
    total_pressure = prims[4] + 0.5 * lax.optimization_barrier(jnp.sum(magnetic * magnetic, axis=0))
    unit_normal = jnp.array([1.0 if component == normal else 0.0 for component in range(3)], dtype=jnp.float32)
    unit_normal = unit_normal.reshape((3,) + (1,) * (velocity.ndim - 1))
    momentum_flux = density * velocity * speed_normal - magnetic * field_normal + unit_normal * total_pressure
    energy_flux = (state[4] + total_pressure) * speed_normal - field_normal * lax.optimization_barrier(jnp.sum(velocity * magnetic, axis=0))
    induction = speed_normal * magnetic - velocity * field_normal
    return jnp.concatenate([(density * speed_normal)[None], momentum_flux, energy_flux[None], induction], axis=0)

def hlle_flux(left, right, normal):
    state_left = conserved(left)
    state_right = conserved(right)
    flux_left = physical_flux(left, state_left, normal)
    flux_right = physical_flux(right, state_right, normal)
    fast_left = fast_speed(left, normal)
    fast_right = fast_speed(right, normal)
    upper = jnp.maximum(jnp.maximum(right[1 + normal] + fast_right, left[1 + normal] + fast_left), 0.0)
    lower = jnp.minimum(jnp.minimum(left[1 + normal] - fast_left, right[1 + normal] - fast_right), 0.0)
    return (upper * flux_left - lower * flux_right + upper * lower * (state_right - state_left)) / (upper - lower)

def minmod(first, second):
    return 0.5 * (jnp.sign(first) + jnp.sign(second)) * jnp.minimum(jnp.abs(first), jnp.abs(second))

def divergence(prims, along, normal):
    backward = trimmed(prims, along, 1, 1) - trimmed(prims, along, 0, 2)
    forward = trimmed(prims, along, 2, 0) - trimmed(prims, along, 1, 1)
    slope = minmod(backward, forward)
    left = trimmed(prims, along, 1, 2) + 0.5 * trimmed(slope, along, 0, 1)
    right = trimmed(prims, along, 2, 1) - 0.5 * trimmed(slope, along, 1, 0)
    flux = hlle_flux(left, right, normal)
    return trimmed(flux, along, 1, 0) - trimmed(flux, along, 0, 1)

def tendency(padded):
    prims = primitive(padded)
    across_x = trimmed(divergence(prims, 1, 0), 2, 2, 2)
    across_y = trimmed(divergence(prims, 2, 1), 1, 2, 2)
    wrapped = jnp.concatenate([prims[..., -2:], prims, prims[..., :2]], axis=3)
    across_z = trimmed(trimmed(divergence(wrapped, 3, 2), 1, 2, 2), 2, 2, 2)
    return -(across_x + across_y + across_z)

def signal_speed(state):
    prims = primitive(state)
    fastest = jnp.abs(prims[1]) + fast_speed(prims, 0)
    fastest = jnp.maximum(fastest, jnp.abs(prims[2]) + fast_speed(prims, 1))
    return jnp.maximum(fastest, jnp.abs(prims[3]) + fast_speed(prims, 2))

def whole_tendency(grid):
    padded = jnp.pad(grid, ((0, 0), (2, 2), (2, 2), (0, 0)), mode='wrap')
    width_x = BRICK_X * BS
    width_y = BRICK_Y * BS
    depth = grid.shape[3]

    def one_brick(index):
        group_index = (index // N_DEV).astype(jnp.int32)
        dev_index = (index % N_DEV).astype(jnp.int32)
        anchor = (jnp.zeros((), jnp.int32), (group_index * width_x).astype(jnp.int32), (dev_index * width_y).astype(jnp.int32), jnp.zeros((), jnp.int32))
        piece = lax.dynamic_slice(padded, anchor, (FIELDS, width_x + 4, width_y + 4, depth))
        return tendency(piece)
    bricks = lax.map(one_brick, jnp.arange(DEVS, dtype=jnp.int32))
    bricks = bricks.reshape(N_GROUP, N_DEV, FIELDS, width_x, width_y, depth)
    return jnp.transpose(bricks, (2, 0, 3, 1, 4, 5)).reshape(grid.shape)

def reference(blocks_in, counts):
    starts = (jnp.cumsum(counts) - counts).astype(jnp.int32)
    curve = jnp.arange(BLOCKS, dtype=jnp.int32)
    owner = (lax.optimization_barrier(jnp.sum((starts[None, :] <= curve[:, None]).astype(jnp.int32), axis=1)) - 1).astype(jnp.int32)
    slot_index = (curve - starts[owner]).astype(jnp.int32)
    live = blocks_in[owner * CAP + slot_index]
    grid = live.reshape(N_GROUP, N_DEV, BRICK_X, BRICK_Y, BRICK_Z, FIELDS, BS, BS, BS)
    grid = jnp.transpose(grid, (5, 0, 2, 6, 1, 3, 7, 4, 8)).reshape(FIELDS, N_GROUP * BRICK_X * BS, N_DEV * BRICK_Y * BS, BRICK_Z * BS)
    step = COURANT / jnp.max(signal_speed(grid))
    first = grid + step * whole_tendency(grid)
    second = 0.5 * (grid + first + step * whole_tendency(first))
    result = second.reshape(FIELDS, N_GROUP, BRICK_X, BS, N_DEV, BRICK_Y, BS, BRICK_Z, BS)
    return jnp.transpose(result, (1, 4, 2, 5, 7, 0, 3, 6, 8)).reshape(BLOCKS, FIELDS, BS * BS * BS)
```

```python
import functools

import jax
import jax.numpy as jnp
from jax import lax
from jax.experimental import pallas as pl
from jax.experimental.pallas import tpu as pltpu
from jax.sharding import PartitionSpec as P

BS = 16
BLK_DEV = 16
FIELDS = 8
XS = 16
TS = 4
CHUNKS = 32
AXES = ("group", "dev")

GAMMA = 5.0 / 3.0
COURANT = 0.25
DENSITY_FLOOR = 0.05
PRESSURE_FLOOR = 0.05
TINY = 1e-37

GRID = (XS, TS, FIELDS, 8, 128)
XFACE = (2, TS, FIELDS, 8, 128)
YFACE = (2, 2, FIELDS, 8, 128)
LIMIT = 40 << 20


def iota(axis):
    return lax.broadcasted_iota(jnp.int32, (8, 128), axis)


def root(value):
    return value * lax.rsqrt(value)


def primitive(state):
    density = jnp.maximum(state[0], DENSITY_FLOOR)
    inverse = 1.0 / density
    velocity = [state[k] * inverse for k in (1, 2, 3)]
    magnetic = state[5:8]
    kinetic = 0.5 * density * (velocity[0] * velocity[0] + velocity[1] * velocity[1] + velocity[2] * velocity[2])
    field = 0.5 * (magnetic[0] * magnetic[0] + magnetic[1] * magnetic[1] + magnetic[2] * magnetic[2])
    pressure = jnp.maximum((GAMMA - 1.0) * (state[4] - kinetic - field), PRESSURE_FLOOR)
    return [density] + velocity + [pressure] + list(magnetic)


def fast_speed(prims, normal, inverse, square):
    magnetic = prims[5:8]
    along = magnetic[normal] * magnetic[normal] * inverse
    sound = (GAMMA * prims[4]) * inverse
    total = sound + square * inverse
    inner = jnp.maximum(total * total - (4.0 * sound) * along, TINY)
    return root(0.5 * (total + root(inner)))


def side(prims, normal):
    density, pressure = prims[0], prims[4]
    velocity, magnetic = prims[1:4], prims[5:8]
    square = magnetic[0] * magnetic[0] + magnetic[1] * magnetic[1] + magnetic[2] * magnetic[2]
    fast = fast_speed(prims, normal, 1.0 / density, square)
    total = pressure + 0.5 * square
    motion = velocity[0] * velocity[0] + velocity[1] * velocity[1] + velocity[2] * velocity[2]
    energy = total + 0.5 * (pressure + density * motion)
    cross = velocity[0] * magnetic[0] + velocity[1] * magnetic[1] + velocity[2] * magnetic[2]
    return fast, total, energy, cross


def weighed(prims, normal, weight, other, total, energy, cross):
    density = prims[0]
    velocity, magnetic = prims[1:4], prims[5:8]
    carried = weight * (velocity[normal] - other)
    bent = weight * magnetic[normal]
    mass = carried * density
    push = weight * total
    momentum = [mass * velocity[k] - bent * magnetic[k] for k in range(3)]
    momentum[normal] = momentum[normal] + push
    power = carried * energy + push * velocity[normal] - bent * cross
    induced = [carried * magnetic[k] - bent * velocity[k] for k in range(3)]
    induced[normal] = -(other * bent)
    return [mass] + momentum + [power] + induced


def hlle(left, right, normal):
    fast_l, total_l, energy_l, cross_l = side(left, normal)
    fast_r, total_r, energy_r, cross_r = side(right, normal)
    speed_l, speed_r = left[1 + normal], right[1 + normal]
    upper = jnp.maximum(jnp.maximum(speed_r + fast_r, speed_l + fast_l), 0.0)
    lower = jnp.minimum(jnp.minimum(speed_l - fast_l, speed_r - fast_r), 0.0)
    weight = upper * (1.0 / (upper - lower))
    part_l = weighed(left, normal, weight, lower, total_l, energy_l, cross_l)
    part_r = weighed(right, normal, 1.0 - weight, upper, total_r, energy_r, cross_r)
    return [a + b for a, b in zip(part_l, part_r)]


def minus(first, second):
    return [a - b for a, b in zip(first, second)]


def plus(first, second):
    return [a + b for a, b in zip(first, second)]


def edges(prims, backward, forward):
    upper, lower = [], []
    for w, a, b in zip(prims, backward, forward):
        half = 0.5 * jnp.maximum(jnp.minimum(a, b), jnp.minimum(jnp.maximum(a, b), 0.0))
        upper.append(w + half)
        lower.append(w - half)
    return upper, lower


def cells(ref, x, t):
    return [ref[x, t, k] for k in range(FIELDS)]


def put(ref, x, t, values):
    for k in range(FIELDS):
        ref[x, t, k] = values[k]


def speed_kernel(count_ref, place_ref, blocks_ref, tile_ref, slots, sems):
    count = count_ref[0]
    depth = 4

    def copy(slot):
        at = slot % depth
        return pltpu.make_async_copy(blocks_ref.at[slot], slots.at[at], sems.at[at])

    for slot in range(depth - 1):
        @pl.when(slot < count)
        def _():
            copy(slot).start()

    def block(slot, top):
        @pl.when(slot + depth - 1 < count)
        def _():
            copy(slot + depth - 1).start()
        copy(slot).wait()
        rows = slots.at[slot % depth].reshape(CHUNKS * FIELDS, 128)
        for part in range(4):
            prims = primitive([rows[pl.ds(part * 64 + k, 8, stride=8), :] for k in range(FIELDS)])
            magnetic = prims[5:8]
            square = magnetic[0] * magnetic[0] + magnetic[1] * magnetic[1] + magnetic[2] * magnetic[2]
            inverse = 1.0 / prims[0]
            for normal in range(3):
                top = jnp.maximum(top, jnp.abs(prims[1 + normal]) + fast_speed(prims, normal, inverse, square))
        return top

    top = lax.fori_loop(0, count, block, jnp.zeros((8, 128), jnp.float32))
    fastest = jnp.max(top)
    counted = jnp.where(iota(1) == place_ref[0], count.astype(jnp.float32), 0.0)
    tile_ref[...] = jnp.where(iota(0) == 0, counted, fastest)


def swapped(value, index, flip):
    value = pltpu.roll(value, 0, 1, stride=16, stride_axis=0)
    value = jnp.take_along_axis(value, index, axis=0, mode="promise_in_bounds")
    value = pltpu.roll(value, 16, 1, stride=16, stride_axis=0)
    return jnp.take_along_axis(value, flip, axis=0, mode="promise_in_bounds")


def swap_indices():
    row, group = iota(0), iota(1) // 16
    flip = 7 - row
    return (group - flip) & 7, flip


def pack_sides(w_ref, xl_ref, xh_ref, yl_ref, yh_ref):
    for layer in range(2):
        for t in range(TS):
            put(xl_ref, layer, t, cells(w_ref, layer, t))
            put(xh_ref, layer, t, cells(w_ref, XS - 2 + layer, t))
    rows = w_ref.reshape(XS * 256, 128)
    for layer in range(2):
        for half in range(2):
            for k in range(FIELDS):
                yl_ref[layer, half, k] = y_layer(rows, half, k, layer)
                yh_ref[layer, half, k] = y_layer(rows, half, k, 30 + layer)


def y_layer(rows, half, k, y):
    return rows[pl.ds(half * 2048 + (y // 8) * 64 + k * 8 + y % 8, 8, stride=256), :]


def assemble_kernel(place_ref, tile_ref, came_ref, own_ref, u_ref, w_ref, xl_ref, xh_ref, yl_ref, yh_ref, slots, sems):
    place = place_ref[0]
    earlier = jnp.where((iota(0) == 0) & (iota(1) < place), tile_ref[...], 0.0)
    surplus = jnp.sum(earlier).astype(jnp.int32) - place * BLK_DEV

    for slot in range(BLK_DEV):
        target = slots.at[slot // 8, :, slot % 8]

        @pl.when(slot < surplus)
        def _():
            source = jnp.clip(BLK_DEV - 1 - surplus + slot, 0, BLK_DEV - 2)
            pltpu.make_async_copy(came_ref.at[source], target, sems.at[slot]).start()

        @pl.when(slot >= surplus)
        def _():
            source = jnp.clip(slot - surplus, 0, BLK_DEV - 1)
            pltpu.make_async_copy(own_ref.at[source], target, sems.at[slot]).start()

    index, flip = swap_indices()
    rows = slots.reshape(2 * CHUNKS * 64, 128)
    for ly in range(2):
        for lz in range(8):
            slot = ly * 8 + lz
            pltpu.make_async_copy(own_ref.at[0], slots.at[ly, :, lz], sems.at[slot]).wait()

        def chunk(c, _):
            state = [swapped(rows[pl.ds((ly * CHUNKS + c) * 64 + k, 8, stride=8), :], index, flip) for k in range(FIELDS)]
            x, t = c // 2, ly * 2 + c % 2
            put(u_ref, x, t, state)
            put(w_ref, x, t, primitive(state))
            return 0

        lax.fori_loop(0, CHUNKS, chunk, 0, unroll=4)
    pack_sides(w_ref, xl_ref, xh_ref, yl_ref, yh_ref)


def inner_kernel(w_ref, out_ref):
    row = iota(0)
    last, first = row == 7, row == 0

    def layer(x, _):
        prims = [cells(w_ref, x, t) for t in range(TS)]
        total = []
        for w in prims:
            forward = [pltpu.roll(v, 127, 1) - v for v in w]
            upper, lower = edges(w, [pltpu.roll(v, 1, 1) for v in forward], forward)
            flux = hlle(upper, [pltpu.roll(v, 127, 1) for v in lower], 2)
            total.append([pltpu.roll(v, 1, 1) - v for v in flux])

        def ahead(values):
            rolled = [[pltpu.roll(v, 7, 0) for v in w] for w in values]
            rolled.append(rolled[-1])
            return [[jnp.where(last, b, a) for a, b in zip(rolled[t], rolled[t + 1])] for t in range(TS)]

        def behind(values):
            rolled = [[pltpu.roll(v, 1, 0) for v in w] for w in values]
            rolled.insert(0, rolled[0])
            return [[jnp.where(first, a, b) for a, b in zip(rolled[t], rolled[t + 1])] for t in range(TS)]

        forward = [minus(a, w) for a, w in zip(ahead(prims), prims)]
        backward = behind(forward)
        both = [edges(w, b, f) for w, b, f in zip(prims, backward, forward)]
        right = ahead([lower for _, lower in both])
        flux = [hlle(both[t][0], right[t], 1) for t in range(TS)]
        flux[0] = [jnp.where(first, 0.0, v) for v in flux[0]]
        flux[3] = [jnp.where(row >= 6, 0.0, v) for v in flux[3]]
        rolled = [[pltpu.roll(v, 1, 0) for v in w] for w in flux]
        for t in range(TS):
            if t == 0:
                before = [jnp.where(first, 0.0, v) for v in rolled[0]]
            else:
                before = [jnp.where(first, a, b) for a, b in zip(rolled[t - 1], rolled[t])]
            put(out_ref, x, t, plus(total[t], minus(before, flux[t])))
        return 0

    lax.fori_loop(0, XS, layer, 0)

    def column(t, _):
        w0, w1, w2, w3 = [cells(w_ref, x, t) for x in range(4)]
        d1, d2 = minus(w2, w1), minus(w3, w2)
        upper, _ = edges(w1, minus(w1, w0), d1)
        after, lower = edges(w2, d1, d2)
        flux = hlle(upper, lower, 0)
        put(out_ref, 1, t, minus(cells(out_ref, 1, t), flux))

        def step(x, carry):
            d, upper, flux = carry
            here, ahead = cells(w_ref, x + 1, t), cells(w_ref, x + 2, t)
            forward = minus(ahead, here)
            after, lower = edges(here, d, forward)
            new = hlle(upper, lower, 0)
            put(out_ref, x, t, plus(cells(out_ref, x, t), minus(flux, new)))
            return forward, after, new

        _, _, flux = lax.fori_loop(2, 14, step, (d2, after, flux))
        put(out_ref, 14, t, plus(cells(out_ref, 14, t), flux))
        return 0

    lax.fori_loop(0, TS, column, 0)


def outer_faces(six, normal):
    ds = [minus(six[i + 1], six[i]) for i in range(len(six) - 1)]
    both = [edges(six[i + 1], ds[i], ds[i + 1]) for i in range(len(six) - 2)]
    return [hlle(both[i][0], both[i + 1][1], normal) for i in range(len(six) - 3)]


def outer(w_ref, sides, xc, yc):
    xl_ref, xh_ref, yl_ref, yh_ref = sides

    def column(t, _):
        near = [cells(xl_ref, 0, t), cells(xl_ref, 1, t)] + [cells(w_ref, x, t) for x in range(3)]
        a, b = outer_faces(near, 0)
        put(xc, 0, t, minus(a, b))
        put(xc, 1, t, b)
        far = [cells(w_ref, x, t) for x in range(13, 16)] + [cells(xh_ref, 0, t), cells(xh_ref, 1, t)]
        a, b = outer_faces(far, 0)
        put(xc, 2, t, [-v for v in a])
        put(xc, 3, t, minus(a, b))
        return 0

    lax.fori_loop(0, TS, column, 0)
    rows = w_ref.reshape(XS * 256, 128)
    packed = yc.reshape(XS * 128, 128)
    zero = jnp.zeros((8, 128), jnp.float32)

    def clear(x, _):
        for part in range(2):
            for k in range(FIELDS):
                yc[x, part, k] = zero
        return 0

    lax.fori_loop(0, XS, clear, 0)

    def store(half, part, y, values):
        for k in range(FIELDS):
            packed[pl.ds(half * 1024 + part * 64 + k * 8 + y, 8, stride=128), :] = values[k]

    for half in range(2):
        own = lambda y: [y_layer(rows, half, k, y) for k in range(FIELDS)]
        sent = lambda ref, layer: [ref[layer, half, k] for k in range(FIELDS)]
        a, b = outer_faces([sent(yl_ref, 0), sent(yl_ref, 1), own(0), own(1), own(2)], 1)
        store(half, 0, 0, minus(a, b))
        store(half, 0, 1, b)
        a, b = outer_faces([own(29), own(30), own(31), sent(yh_ref, 0), sent(yh_ref, 1)], 1)
        store(half, 1, 6, [-v for v in a])
        store(half, 1, 7, minus(a, b))


def changes(t_ref, xc, yc, x, t, edge):
    total = cells(t_ref, x, t)
    if t in (0, 3):
        total = plus(total, cells(yc, x, t // 3))
    if edge is not None:
        total = plus(total, cells(xc, edge, t))
    return total


def each_layer(work):
    for edge, x in enumerate((0, 1, XS - 2, XS - 1)):
        work(x, edge)
    lax.fori_loop(2, XS - 2, lambda x, _: (work(x, None), 0)[1], 0)


def step_of(tile_ref):
    return COURANT / jnp.max(jnp.where(iota(0) == 1, tile_ref[...], 0.0))


def first_kernel(tile_ref, w_ref, u_ref, t_ref, xl, xh, yl, yh, s_ref, w2_ref, xl_ref, xh_ref, yl_ref, yh_ref, xc, yc):
    step = step_of(tile_ref)
    outer(w_ref, (xl, xh, yl, yh), xc, yc)

    def work(x, edge):
        for t in range(TS):
            change = changes(t_ref, xc, yc, x, t, edge)
            state = cells(u_ref, x, t)
            first = [u + step * c for u, c in zip(state, change)]
            put(s_ref, x, t, [0.5 * (u + f) for u, f in zip(state, first)])
            put(w2_ref, x, t, primitive(first))

    each_layer(work)
    pack_sides(w2_ref, xl_ref, xh_ref, yl_ref, yh_ref)


def second_kernel(tile_ref, w_ref, s_ref, t_ref, xl, xh, yl, yh, out_ref, xc, yc):
    step = 0.5 * step_of(tile_ref)
    outer(w_ref, (xl, xh, yl, yh), xc, yc)
    index, flip = swap_indices()
    rows = out_ref.reshape(BLK_DEV * CHUNKS * FIELDS, 128)

    def work(x, edge):
        for t in range(TS):
            change = changes(t_ref, xc, yc, x, t, edge)
            chunk = 2 * x + t % 2
            for k, (s, c) in enumerate(zip(cells(s_ref, x, t), change)):
                start = ((t // 2) * 8 * CHUNKS + chunk) * 8 + k
                rows[pl.ds(start, 8, stride=CHUNKS * 8), :] = swapped(s + step * c, index, flip)

    each_layer(work)


VMEM = pl.BlockSpec(memory_space=pltpu.VMEM)
SMEM = pl.BlockSpec(memory_space=pltpu.SMEM)
ANY = pl.BlockSpec(memory_space=pl.ANY)


def shape(dims):
    return jax.ShapeDtypeStruct(dims, jnp.float32)


def kernel(function, in_specs, outs, scratch, name, flops):
    single = not isinstance(outs, list)
    return pl.pallas_call(
        function,
        out_shape=shape(outs) if single else [shape(dims) for dims in outs],
        in_specs=in_specs,
        out_specs=VMEM if single else [VMEM] * len(outs),
        scratch_shapes=scratch,
        name=name,
        compiler_params=pltpu.CompilerParams(vmem_limit_bytes=LIMIT),
        cost_estimate=pl.CostEstimate(flops=flops, bytes_accessed=6 << 20, transcendentals=0),
    )


def shifted(value, axis, by):
    count = lax.axis_size(axis)
    return lax.ppermute(value, axis, [(i, (i + by) % count) for i in range(count)])


def exchanged(xl, xh, yl, yh):
    return shifted(xh, "group", 1), shifted(xl, "group", -1), shifted(yh, "dev", 1), shifted(yl, "dev", -1)


def body(blocks_in, counts):
    devices = lax.axis_size(AXES)
    place = lax.axis_index(AXES).astype(jnp.int32).reshape(1)
    slots = blocks_in.shape[0]
    padded = jnp.concatenate([jnp.zeros((BLK_DEV - 1,) + blocks_in.shape[1:], jnp.float32), blocks_in], axis=0)
    outgoing = lax.dynamic_slice_in_dim(padded, counts[0], BLK_DEV - 1, 0)
    came = lax.ppermute(outgoing, AXES, [(i, i + 1) for i in range(devices - 1)])
    tiles = lambda value: value.reshape(value.shape[0], FIELDS, CHUNKS, 128).swapaxes(1, 2)
    own = tiles(blocks_in)
    tile = kernel(
        speed_kernel,
        [SMEM, SMEM, ANY],
        (8, 128),
        [pltpu.VMEM((4, CHUNKS, FIELDS, 128), jnp.float32), pltpu.SemaphoreType.DMA((4,))],
        "signal_speed",
        1 << 20,
    )(counts, place, own)
    distance = 1
    while distance < devices:
        tile = jnp.maximum(tile, lax.ppermute(tile, AXES, [(i, i ^ distance) for i in range(devices)]))
        distance *= 2
    sides = [XFACE, XFACE, YFACE, YFACE]
    u, w, *faces = kernel(
        assemble_kernel,
        [SMEM, VMEM, ANY, ANY],
        [GRID, GRID] + sides,
        [pltpu.VMEM((2, CHUNKS, 8, FIELDS, 128), jnp.float32), pltpu.SemaphoreType.DMA((BLK_DEV,))],
        "assemble",
        1 << 20,
    )(place, tile, tiles(came), own)
    corrections = [pltpu.VMEM((4, TS, FIELDS, 8, 128), jnp.float32), pltpu.VMEM((XS, 2, FIELDS, 8, 128), jnp.float32)]
    inner = kernel(inner_kernel, [VMEM], GRID, [], "inner_fluxes", 40 << 20)
    ghosts = exchanged(*faces)
    s, w2, *faces = kernel(first_kernel, [VMEM] * 8, [GRID, GRID] + sides, corrections, "first_stage", 1 << 20)(
        tile, w, u, inner(w), *ghosts
    )
    ghosts = exchanged(*faces)
    out = kernel(second_kernel, [VMEM] * 8, (BLK_DEV, CHUNKS, FIELDS, 128), corrections, "second_stage", 1 << 20)(
        tile, w2, s, inner(w2), *ghosts
    )
    return out.swapaxes(1, 2).reshape(BLK_DEV, FIELDS, BS * BS * BS)


def solution(mesh):
    in_specs = (P(AXES, None, None), P(AXES))
    out_specs = P(AXES, None, None)
    return jax.shard_map(body, mesh=mesh, in_specs=in_specs, out_specs=out_specs, check_vma=False)
```

```python
import functools

import jax
import jax.numpy as jnp
from jax import lax
from jax.experimental import pallas as pl
from jax.experimental.pallas import tpu as pltpu
from jax.sharding import PartitionSpec as P

BS = 16
BLK_DEV = 16
FIELDS = 8
XS = 16
TS = 4
CHUNKS = 32
AXES = ("group", "dev")
ROUNDS = ((2, 32), (6, 96), (8, 32), (24, 96), (32, 32), (96, 96))

GAMMA = 5.0 / 3.0
COURANT = 0.25
DENSITY_FLOOR = 0.05
PRESSURE_FLOOR = 0.05
TINY = 1e-37

GRID = (XS, TS, FIELDS, 8, 128)
XFACE = (2, TS, FIELDS, 8, 128)
YFACE = (2, 2, FIELDS, 8, 128)
LIMIT = 24 << 20
ALL = 57 << 20


def iota(axis):
    return lax.broadcasted_iota(jnp.int32, (8, 128), axis)


def root(value):
    return value * lax.rsqrt(value)


def primitive(state):
    density = jnp.maximum(state[0], DENSITY_FLOOR)
    inverse = 1.0 / density
    velocity = [state[k] * inverse for k in (1, 2, 3)]
    magnetic = state[5:8]
    kinetic = 0.5 * density * (velocity[0] * velocity[0] + velocity[1] * velocity[1] + velocity[2] * velocity[2])
    field = 0.5 * (magnetic[0] * magnetic[0] + magnetic[1] * magnetic[1] + magnetic[2] * magnetic[2])
    pressure = jnp.maximum((GAMMA - 1.0) * (state[4] - kinetic - field), PRESSURE_FLOOR)
    return [density] + velocity + [pressure] + list(magnetic)


def fast_speed(prims, normal, inverse, square):
    magnetic = prims[5:8]
    along = magnetic[normal] * magnetic[normal] * inverse
    sound = (GAMMA * prims[4]) * inverse
    total = sound + square * inverse
    inner = jnp.maximum(total * total - (4.0 * sound) * along, TINY)
    return root(0.5 * (total + root(inner)))


def side(prims, normal):
    density, pressure = prims[0], prims[4]
    velocity, magnetic = prims[1:4], prims[5:8]
    square = magnetic[0] * magnetic[0] + magnetic[1] * magnetic[1] + magnetic[2] * magnetic[2]
    fast = fast_speed(prims, normal, 1.0 / density, square)
    total = pressure + 0.5 * square
    motion = velocity[0] * velocity[0] + velocity[1] * velocity[1] + velocity[2] * velocity[2]
    energy = total + 0.5 * (pressure + density * motion)
    cross = velocity[0] * magnetic[0] + velocity[1] * magnetic[1] + velocity[2] * magnetic[2]
    return fast, total, energy, cross


def weighed(prims, normal, weight, other, total, energy, cross):
    density = prims[0]
    velocity, magnetic = prims[1:4], prims[5:8]
    carried = weight * (velocity[normal] - other)
    bent = weight * magnetic[normal]
    mass = carried * density
    push = weight * total
    momentum = [mass * velocity[k] - bent * magnetic[k] for k in range(3)]
    momentum[normal] = momentum[normal] + push
    power = carried * energy + push * velocity[normal] - bent * cross
    induced = [carried * magnetic[k] - bent * velocity[k] for k in range(3)]
    induced[normal] = -(other * bent)
    return [mass] + momentum + [power] + induced


def hlle(left, right, normal):
    fast_l, total_l, energy_l, cross_l = side(left, normal)
    fast_r, total_r, energy_r, cross_r = side(right, normal)
    speed_l, speed_r = left[1 + normal], right[1 + normal]
    upper = jnp.maximum(jnp.maximum(speed_r + fast_r, speed_l + fast_l), 0.0)
    lower = jnp.minimum(jnp.minimum(speed_l - fast_l, speed_r - fast_r), 0.0)
    weight = upper * (1.0 / (upper - lower))
    part_l = weighed(left, normal, weight, lower, total_l, energy_l, cross_l)
    part_r = weighed(right, normal, 1.0 - weight, upper, total_r, energy_r, cross_r)
    return [a + b for a, b in zip(part_l, part_r)]


def minus(first, second):
    return [a - b for a, b in zip(first, second)]


def plus(first, second):
    return [a + b for a, b in zip(first, second)]


def edges(prims, backward, forward):
    upper, lower = [], []
    for w, a, b in zip(prims, backward, forward):
        half = 0.5 * jnp.maximum(jnp.minimum(a, b), jnp.minimum(jnp.maximum(a, b), 0.0))
        upper.append(w + half)
        lower.append(w - half)
    return upper, lower


def cells(ref, x, t):
    return [ref[x, t, k] for k in range(FIELDS)]


def put(ref, x, t, values):
    for k in range(FIELDS):
        ref[x, t, k] = values[k]


def depart_kernel(count_ref, place_ref, blocks_ref, out_ref, tile_ref, slots, out_sems, sems):
    count, places = count_ref[0], BLK_DEV - 1
    group = 4
    groups = pl.cdiv(blocks_ref.shape[0], group)

    def outgoing(work):
        @pl.when(count >= places)
        def _():
            first = jnp.clip(count - places, 0, blocks_ref.shape[0] - places)
            work(pltpu.make_async_copy(blocks_ref.at[pl.ds(first, places)], out_ref, out_sems.at[0]))

        for place in range(1, places):
            slot = count - places + place

            @pl.when((count < places) & (slot >= 0))
            def _():
                source = jnp.clip(slot, 0, places)
                work(pltpu.make_async_copy(blocks_ref.at[source], out_ref.at[place], out_sems.at[place]))

    def incoming(index, work):
        size = min(group, blocks_ref.shape[0] - index * group)
        part = pl.ds(index * group, size)

        @pl.when(index * group < count)
        def _():
            work(pltpu.make_async_copy(blocks_ref.at[part], slots.at[part], sems.at[index]))

    for index in range(groups):
        incoming(index, lambda copy: copy.start())
        if index == 0:
            outgoing(lambda copy: copy.start())

    rows = slots.reshape(slots.shape[0] * CHUNKS * FIELDS, 128)

    def speeds(start, tops):
        prims = primitive([rows[pl.ds(start + k, 8, stride=8), :] for k in range(FIELDS)])
        magnetic = prims[5:8]
        square = magnetic[0] * magnetic[0] + magnetic[1] * magnetic[1] + magnetic[2] * magnetic[2]
        inverse = 1.0 / prims[0]
        for normal in range(3):
            speed = jnp.abs(prims[1 + normal]) + fast_speed(prims, normal, inverse, square)
            tops[normal] = jnp.maximum(tops[normal], speed)

    def several(index, tops):
        for which in range(groups):
            @pl.when(index == which)
            def _():
                incoming(which, lambda copy: copy.wait())
        tops = list(tops)
        for which in range(group):
            slot = jnp.minimum(index * group + which, count - 1)
            for part in range(4):
                speeds(slot * (CHUNKS * FIELDS) + part * 64, tops)
        return tuple(tops)

    tops = lax.fori_loop(0, pl.cdiv(count, group), several, (jnp.zeros((8, 128), jnp.float32),) * 3)
    fastest = jnp.max(jnp.maximum(jnp.maximum(tops[0], tops[1]), tops[2]))
    counted = jnp.where(iota(1) == place_ref[0], count.astype(jnp.float32), 0.0)
    tile_ref[...] = jnp.where(iota(0) == 0, counted, fastest)
    outgoing(lambda copy: copy.wait())


def swapped(value, index, flip):
    value = pltpu.roll(value, 0, 1, stride=16, stride_axis=0)
    value = jnp.take_along_axis(value, index, axis=0, mode="promise_in_bounds")
    value = pltpu.roll(value, 16, 1, stride=16, stride_axis=0)
    return jnp.take_along_axis(value, flip, axis=0, mode="promise_in_bounds")


def swap_indices():
    row, group = iota(0), iota(1) // 16
    flip = 7 - row
    return (group - flip) & 7, flip


def pack_sides(core, w_ref, xl_ref, xh_ref, yn_ref, yf_ref):
    for layer in range(2):
        for t in range(TS):
            put(xl_ref, layer, t, cells(w_ref, layer, t))
            put(xh_ref, layer, t, cells(w_ref, XS - 2 + layer, t))
    rows = w_ref.reshape(XS * 256, 128)
    high = y_offset(30)
    for layer in range(2):
        for half in range(2):
            for k in range(FIELDS):
                start = half * 2048 + k * 8 + layer
                yn_ref[layer, half, k] = rows[pl.ds(start + (1 - core) * high, 8, stride=256), :]
                yf_ref[layer, half, k] = rows[pl.ds(start + core * high, 8, stride=256), :]


def y_offset(y):
    return (y // 8) * 64 + y % 8


def y_layer(rows, half, k, y):
    return rows[pl.ds(half * 2048 + k * 8 + y_offset(y), 8, stride=256), :]


def assemble_kernel(place_ref, tile_ref, came_ref, own_ref, u_ref, w_ref, xl_ref, xh_ref, yn_ref, yf_ref, slots, sems):
    place = place_ref[0]
    earlier = jnp.where((iota(0) == 0) & (iota(1) < place), tile_ref[...], 0.0)
    surplus = jnp.sum(earlier).astype(jnp.int32) - place * BLK_DEV

    for slot in range(BLK_DEV):
        target = slots.at[slot // 8, :, slot % 8]

        @pl.when(slot < surplus)
        def _():
            source = jnp.clip(BLK_DEV - 1 - surplus + slot, 0, BLK_DEV - 2)
            pltpu.make_async_copy(came_ref.at[source], target, sems.at[slot]).start()

        @pl.when(slot >= surplus)
        def _():
            source = jnp.clip(slot - surplus, 0, BLK_DEV - 1)
            pltpu.make_async_copy(own_ref.at[source], target, sems.at[slot]).start()

    index, flip = swap_indices()
    rows = slots.reshape(2 * CHUNKS * 64, 128)
    for ly in range(2):
        for lz in range(8):
            slot = ly * 8 + lz
            pltpu.make_async_copy(own_ref.at[0], slots.at[ly, :, lz], sems.at[slot]).wait()

        def chunk(c, _):
            state = [swapped(rows[pl.ds((ly * CHUNKS + c) * 64 + k, 8, stride=8), :], index, flip) for k in range(FIELDS)]
            x, t = c // 2, ly * 2 + c % 2
            put(u_ref, x, t, state)
            put(w_ref, x, t, primitive(state))
            return 0

        lax.fori_loop(0, CHUNKS, chunk, 0, unroll=4)
    pack_sides(place % 2, w_ref, xl_ref, xh_ref, yn_ref, yf_ref)


def inner_kernel(w_ref, x_ref, y_ref, z_ref):
    row = iota(0)
    last, first = row == 7, row == 0

    def along_z(i, _):
        x, t = i // TS, i % TS
        w = cells(w_ref, x, t)
        forward = [pltpu.roll(v, 127, 1) - v for v in w]
        upper, lower = edges(w, [pltpu.roll(v, 1, 1) for v in forward], forward)
        flux = hlle(upper, [pltpu.roll(v, 127, 1) for v in lower], 2)
        put(z_ref, x, t, [pltpu.roll(v, 1, 1) - v for v in flux])
        return 0

    lax.fori_loop(0, XS * TS, along_z, 0, unroll=8)

    def ahead(values):
        rolled = [[pltpu.roll(v, 7, 0) for v in w] for w in values]
        rolled.append(rolled[-1])
        return [[jnp.where(last, b, a) for a, b in zip(rolled[t], rolled[t + 1])] for t in range(TS)]

    def behind(values):
        rolled = [[pltpu.roll(v, 1, 0) for v in w] for w in values]
        rolled.insert(0, rolled[0])
        return [[jnp.where(first, a, b) for a, b in zip(rolled[t], rolled[t + 1])] for t in range(TS)]

    def along_y(x, _):
        prims = [cells(w_ref, x, t) for t in range(TS)]
        forward = [minus(a, w) for a, w in zip(ahead(prims), prims)]
        backward = behind(forward)
        both = [edges(w, b, f) for w, b, f in zip(prims, backward, forward)]
        right = ahead([lower for _, lower in both])
        flux = [hlle(both[t][0], right[t], 1) for t in range(TS)]
        flux[0] = [jnp.where(first, 0.0, v) for v in flux[0]]
        flux[3] = [jnp.where(row >= 6, 0.0, v) for v in flux[3]]
        rolled = [[pltpu.roll(v, 1, 0) for v in w] for w in flux]
        for t in range(TS):
            if t == 0:
                before = [jnp.where(first, 0.0, v) for v in rolled[0]]
            else:
                before = [jnp.where(first, a, b) for a, b in zip(rolled[t - 1], rolled[t])]
            put(y_ref, x, t, minus(before, flux[t]))
        return 0

    lax.fori_loop(0, XS, along_y, 0)

    def along_x(pair, _):
        both = (2 * pair, 2 * pair + 1)
        start = []
        for t in both:
            w0, w1, w2, w3 = [cells(w_ref, x, t) for x in range(4)]
            d1, d2 = minus(w2, w1), minus(w3, w2)
            upper, _ = edges(w1, minus(w1, w0), d1)
            after, lower = edges(w2, d1, d2)
            flux = hlle(upper, lower, 0)
            put(x_ref, 1, t, [-v for v in flux])
            start.append((d2, after, flux))

        def step(x, carry):
            result = []
            for t, (d, upper, flux) in zip(both, carry):
                here, beyond = cells(w_ref, x + 1, t), cells(w_ref, x + 2, t)
                forward = minus(beyond, here)
                after, lower = edges(here, d, forward)
                new = hlle(upper, lower, 0)
                put(x_ref, x, t, minus(flux, new))
                result.append((forward, after, new))
            return result

        for t, (_, _, flux) in zip(both, lax.fori_loop(2, 14, step, start)):
            put(x_ref, 14, t, flux)
        return 0

    lax.fori_loop(0, TS // 2, along_x, 0)


def outer_faces(six, normal):
    ds = [minus(six[i + 1], six[i]) for i in range(len(six) - 1)]
    both = [edges(six[i + 1], ds[i], ds[i + 1]) for i in range(len(six) - 2)]
    return [hlle(both[i][0], both[i + 1][1], normal) for i in range(len(six) - 3)]


def outer(core, w_ref, sides, xc, yc):
    xl_ref, xh_ref, yn_ref, yf_ref = sides

    def column(t, _):
        near = [cells(xl_ref, 0, t), cells(xl_ref, 1, t)] + [cells(w_ref, x, t) for x in range(3)]
        a, b = outer_faces(near, 0)
        put(xc, 0, t, minus(a, b))
        put(xc, 1, t, b)
        far = [cells(w_ref, x, t) for x in range(13, 16)] + [cells(xh_ref, 0, t), cells(xh_ref, 1, t)]
        a, b = outer_faces(far, 0)
        put(xc, 2, t, [-v for v in a])
        put(xc, 3, t, minus(a, b))
        return 0

    lax.fori_loop(0, TS, column, 0)
    rows = w_ref.reshape(XS * 256, 128)
    packed = yc.reshape(XS * 128, 128)
    zero = jnp.zeros((8, 128), jnp.float32)

    def clear(x, _):
        for part in range(2):
            for k in range(FIELDS):
                yc[x, part, k] = zero
        return 0

    lax.fori_loop(0, XS, clear, 0)

    def store(half, part, y, values):
        for k in range(FIELDS):
            packed[pl.ds(half * 1024 + part * 64 + k * 8 + y, 8, stride=128), :] = values[k]

    for half in range(2):
        own = lambda y: [y_layer(rows, half, k, y) for k in range(FIELDS)]
        sent = lambda layer, near: [jnp.where(near, yn_ref[layer, half, k], yf_ref[layer, half, k]) for k in range(FIELDS)]
        a, b = outer_faces([sent(0, core == 1), sent(1, core == 1), own(0), own(1), own(2)], 1)
        store(half, 0, 0, minus(a, b))
        store(half, 0, 1, b)
        a, b = outer_faces([own(29), own(30), own(31), sent(0, core == 0), sent(1, core == 0)], 1)
        store(half, 1, 6, [-v for v in a])
        store(half, 1, 7, minus(a, b))


def changes(inner, xc, yc, x, t, edge):
    x_ref, y_ref, z_ref = inner
    total = plus(cells(y_ref, x, t), cells(z_ref, x, t))
    if edge not in (0, 3):
        total = plus(total, cells(x_ref, x, t))
    if t in (0, 3):
        total = plus(total, cells(yc, x, t // 3))
    if edge is not None:
        total = plus(total, cells(xc, edge, t))
    return total


def each_layer(work):
    for edge, x in enumerate((0, 1, XS - 2, XS - 1)):
        work(x, edge)
    lax.fori_loop(2, XS - 2, lambda x, _: (work(x, None), 0)[1], 0)


def step_of(tile_ref):
    return COURANT / jnp.max(jnp.where(iota(0) == 1, tile_ref[...], 0.0))


def first_kernel(place_ref, tile_ref, w_ref, u_ref, tx, ty, tz, xl, xh, yn, yf, s_ref, w2_ref, xl_ref, xh_ref, yn_ref, yf_ref, xc, yc):
    step = step_of(tile_ref)
    core = place_ref[0] % 2
    outer(core, w_ref, (xl, xh, yn, yf), xc, yc)

    def work(x, edge):
        for t in range(TS):
            change = changes((tx, ty, tz), xc, yc, x, t, edge)
            state = cells(u_ref, x, t)
            first = [u + step * c for u, c in zip(state, change)]
            put(s_ref, x, t, [0.5 * (u + f) for u, f in zip(state, first)])
            put(w2_ref, x, t, primitive(first))

    each_layer(work)
    pack_sides(core, w2_ref, xl_ref, xh_ref, yn_ref, yf_ref)


def second_kernel(place_ref, tile_ref, w_ref, s_ref, tx, ty, tz, xl, xh, yn, yf, out_ref, xc, yc):
    step = 0.5 * step_of(tile_ref)
    outer(place_ref[0] % 2, w_ref, (xl, xh, yn, yf), xc, yc)
    index, flip = swap_indices()
    rows = out_ref.reshape(BLK_DEV * CHUNKS * FIELDS, 128)

    def work(x, edge):
        for t in range(TS):
            change = changes((tx, ty, tz), xc, yc, x, t, edge)
            chunk = 2 * x + t % 2
            for k, (s, c) in enumerate(zip(cells(s_ref, x, t), change)):
                start = ((t // 2) * 8 * CHUNKS + chunk) * 8 + k
                rows[pl.ds(start, 8, stride=CHUNKS * 8), :] = swapped(s + step * c, index, flip)

    each_layer(work)


VMEM = pl.BlockSpec(memory_space=pltpu.VMEM)
SMEM = pl.BlockSpec(memory_space=pltpu.SMEM)
ANY = pl.BlockSpec(memory_space=pl.ANY)
HBM = pl.BlockSpec(memory_space=pltpu.HBM)


def shape(dims):
    return jax.ShapeDtypeStruct(dims, jnp.float32)


def kernel(function, in_specs, outs, scratch, name, flops, limit=LIMIT):
    single = not isinstance(outs, list)
    return pl.pallas_call(
        function,
        out_shape=shape(outs) if single else [shape(dims) for dims in outs],
        in_specs=in_specs,
        out_specs=VMEM if single else [VMEM] * len(outs),
        scratch_shapes=scratch,
        name=name,
        compiler_params=pltpu.CompilerParams(vmem_limit_bytes=limit),
        cost_estimate=pl.CostEstimate(flops=flops, bytes_accessed=6 << 20, transcendentals=0),
    )


def shifted(value, axis, by):
    count = lax.axis_size(axis)
    return lax.ppermute(value, axis, [(i, (i + by) % count) for i in range(count)])


def exchanged(xl, xh, yn, yf):
    count = lax.axis_size("dev")
    near = [(i, i ^ 1) for i in range(count)]
    far = [(i, (i + 1) % count if i % 2 else (i - 1) % count) for i in range(count)]
    return shifted(xh, "group", 1), shifted(xl, "group", -1), lax.ppermute(yn, "dev", near), lax.ppermute(yf, "dev", far)


def body(blocks_in, counts):
    devices = lax.axis_size(AXES)
    place = lax.axis_index(AXES).astype(jnp.int32).reshape(1)
    tiles = lambda value: value.reshape(value.shape[0], FIELDS, CHUNKS, 128).swapaxes(1, 2)
    own = tiles(blocks_in)
    passed = (BLK_DEV - 1, CHUNKS, FIELDS, 128)
    outgoing, tile = kernel(
        depart_kernel,
        [SMEM, SMEM, HBM],
        [passed, (8, 128)],
        [
            pltpu.VMEM((blocks_in.shape[0], CHUNKS, FIELDS, 128), jnp.float32),
            pltpu.SemaphoreType.DMA((BLK_DEV - 1,)),
            pltpu.SemaphoreType.DMA((pl.cdiv(blocks_in.shape[0], 4),)),
        ],
        "depart",
        1 << 20,
        ALL,
    )(counts, place, own)
    came = lax.ppermute(outgoing, AXES, [(i, i + 1) for i in range(devices - 1)])
    tile = jnp.maximum(tile, lax.ppermute(tile, AXES, [(i, i ^ 1) for i in range(devices)]))
    for masks in ROUNDS:
        tile = jnp.maximum(tile, lax.ppermute(tile, AXES, [(i, i ^ masks[i % 2]) for i in range(devices)]))
    tile = jnp.maximum(tile, lax.ppermute(tile, AXES, [(i, i ^ 1) for i in range(devices)]))
    sides = [XFACE, XFACE, YFACE, YFACE]
    u, w, *faces = kernel(
        assemble_kernel,
        [SMEM, VMEM, ANY, ANY],
        [GRID, GRID] + sides,
        [pltpu.VMEM((2, CHUNKS, 8, FIELDS, 128), jnp.float32), pltpu.SemaphoreType.DMA((BLK_DEV,))],
        "assemble",
        1 << 20,
    )(place, tile, came, own)
    corrections = [pltpu.VMEM((4, TS, FIELDS, 8, 128), jnp.float32), pltpu.VMEM((XS, 2, FIELDS, 8, 128), jnp.float32)]
    inner = kernel(inner_kernel, [VMEM], [GRID] * 3, [], "inner_fluxes", 40 << 20)
    specs = [SMEM] + [VMEM] * 10
    ghosts = exchanged(*faces)
    s, w2, *faces = kernel(first_kernel, specs, [GRID, GRID] + sides, corrections, "first_stage", 1 << 20)(
        place, tile, w, u, *inner(w), *ghosts
    )
    ghosts = exchanged(*faces)
    out = kernel(second_kernel, specs, (BLK_DEV, CHUNKS, FIELDS, 128), corrections, "second_stage", 1 << 20)(
        place, tile, w2, s, *inner(w2), *ghosts
    )
    return out.swapaxes(1, 2).reshape(BLK_DEV, FIELDS, BS * BS * BS)


def solution(mesh):
    in_specs = (P(AXES, None, None), P(AXES))
    out_specs = P(AXES, None, None)
    return jax.shard_map(body, mesh=mesh, in_specs=in_specs, out_specs=out_specs, check_vma=False)
```

```python
import functools

import jax
import jax.numpy as jnp
from jax import lax
from jax.experimental import pallas as pl
from jax.experimental.pallas import tpu as pltpu
from jax.sharding import PartitionSpec as P

BS = 16
BLK_DEV = 16
FIELDS = 8
XS = 16
TS = 4
CHUNKS = 32
AXES = ("group", "dev")
ROUNDS = ((2, 32), (6, 96), (8, 32), (24, 96), (32, 32), (96, 96))

GAMMA = 5.0 / 3.0
COURANT = 0.25
DENSITY_FLOOR = 0.05
PRESSURE_FLOOR = 0.05
TINY = 1e-37

GRID = (XS, TS, FIELDS, 8, 128)
XFACE = (2, TS, FIELDS, 8, 128)
YFACE = (2, 2, FIELDS, 8, 128)
LIMIT = 24 << 20


def iota(axis):
    return lax.broadcasted_iota(jnp.int32, (8, 128), axis)


def root(value):
    return value * lax.rsqrt(value)


def primitive(state):
    density = jnp.maximum(state[0], DENSITY_FLOOR)
    inverse = 1.0 / density
    velocity = [state[k] * inverse for k in (1, 2, 3)]
    magnetic = state[5:8]
    kinetic = 0.5 * density * (velocity[0] * velocity[0] + velocity[1] * velocity[1] + velocity[2] * velocity[2])
    field = 0.5 * (magnetic[0] * magnetic[0] + magnetic[1] * magnetic[1] + magnetic[2] * magnetic[2])
    pressure = jnp.maximum((GAMMA - 1.0) * (state[4] - kinetic - field), PRESSURE_FLOOR)
    return [density] + velocity + [pressure] + list(magnetic)


def fast_speed(prims, normal, inverse, square):
    magnetic = prims[5:8]
    along = magnetic[normal] * magnetic[normal] * inverse
    sound = (GAMMA * prims[4]) * inverse
    total = sound + square * inverse
    inner = jnp.maximum(total * total - (4.0 * sound) * along, TINY)
    return root(0.5 * (total + root(inner)))


def side(prims, normal):
    density, pressure = prims[0], prims[4]
    velocity, magnetic = prims[1:4], prims[5:8]
    square = magnetic[0] * magnetic[0] + magnetic[1] * magnetic[1] + magnetic[2] * magnetic[2]
    fast = fast_speed(prims, normal, 1.0 / density, square)
    total = pressure + 0.5 * square
    motion = velocity[0] * velocity[0] + velocity[1] * velocity[1] + velocity[2] * velocity[2]
    energy = total + 0.5 * (pressure + density * motion)
    cross = velocity[0] * magnetic[0] + velocity[1] * magnetic[1] + velocity[2] * magnetic[2]
    return fast, total, energy, cross


def weighed(prims, normal, weight, other, total, energy, cross):
    density = prims[0]
    velocity, magnetic = prims[1:4], prims[5:8]
    carried = weight * (velocity[normal] - other)
    bent = weight * magnetic[normal]
    mass = carried * density
    push = weight * total
    momentum = [mass * velocity[k] - bent * magnetic[k] for k in range(3)]
    momentum[normal] = momentum[normal] + push
    power = carried * energy + push * velocity[normal] - bent * cross
    induced = [carried * magnetic[k] - bent * velocity[k] for k in range(3)]
    induced[normal] = -(other * bent)
    return [mass] + momentum + [power] + induced


def hlle(left, right, normal):
    fast_l, total_l, energy_l, cross_l = side(left, normal)
    fast_r, total_r, energy_r, cross_r = side(right, normal)
    speed_l, speed_r = left[1 + normal], right[1 + normal]
    upper = jnp.maximum(jnp.maximum(speed_r + fast_r, speed_l + fast_l), 0.0)
    lower = jnp.minimum(jnp.minimum(speed_l - fast_l, speed_r - fast_r), 0.0)
    weight = upper * (1.0 / (upper - lower))
    part_l = weighed(left, normal, weight, lower, total_l, energy_l, cross_l)
    part_r = weighed(right, normal, 1.0 - weight, upper, total_r, energy_r, cross_r)
    return [a + b for a, b in zip(part_l, part_r)]


def minus(first, second):
    return [a - b for a, b in zip(first, second)]


def plus(first, second):
    return [a + b for a, b in zip(first, second)]


def edges(prims, backward, forward):
    upper, lower = [], []
    for w, a, b in zip(prims, backward, forward):
        half = 0.5 * jnp.maximum(jnp.minimum(a, b), jnp.minimum(jnp.maximum(a, b), 0.0))
        upper.append(w + half)
        lower.append(w - half)
    return upper, lower


def cells(ref, x, t):
    return [ref[x, t, k] for k in range(FIELDS)]


def put(ref, x, t, values):
    for k in range(FIELDS):
        ref[x, t, k] = values[k]


def outgoing_kernel(count_ref, blocks_ref, out_ref, sems):
    count, places = count_ref[0], BLK_DEV - 1

    def each(work):
        for place in range(places):
            slot = count - places + place

            @pl.when(slot >= 0)
            def _():
                source = jnp.clip(slot, 0, blocks_ref.shape[0] - 1)
                work(pltpu.make_async_copy(blocks_ref.at[source], out_ref.at[place], sems.at[place]))

    each(lambda copy: copy.start())
    each(lambda copy: copy.wait())


def speed_kernel(count_ref, place_ref, blocks_ref, tile_ref, slots, sems):
    count = count_ref[0]
    group = 4
    groups = pl.cdiv(blocks_ref.shape[0], group)

    def incoming(index, work):
        size = min(group, blocks_ref.shape[0] - index * group)
        part = pl.ds(index * group, size)

        @pl.when(index * group < count)
        def _():
            work(pltpu.make_async_copy(blocks_ref.at[part], slots.at[part], sems.at[index]))

    for index in range(groups):
        incoming(index, lambda copy: copy.start())

    rows = slots.reshape(slots.shape[0] * CHUNKS * FIELDS, 128)

    def speeds(start, tops):
        prims = primitive([rows[pl.ds(start + k, 8, stride=8), :] for k in range(FIELDS)])
        magnetic = prims[5:8]
        square = magnetic[0] * magnetic[0] + magnetic[1] * magnetic[1] + magnetic[2] * magnetic[2]
        inverse = 1.0 / prims[0]
        for normal in range(3):
            speed = jnp.abs(prims[1 + normal]) + fast_speed(prims, normal, inverse, square)
            tops[normal] = jnp.maximum(tops[normal], speed)

    def several(index, tops):
        for which in range(groups):
            @pl.when(index == which)
            def _():
                incoming(which, lambda copy: copy.wait())
        tops = list(tops)
        for which in range(group):
            slot = jnp.minimum(index * group + which, count - 1)
            for part in range(4):
                speeds(slot * (CHUNKS * FIELDS) + part * 64, tops)
        return tuple(tops)

    tops = lax.fori_loop(0, pl.cdiv(count, group), several, (jnp.zeros((8, 128), jnp.float32),) * 3)
    fastest = jnp.max(jnp.maximum(jnp.maximum(tops[0], tops[1]), tops[2]))
    counted = jnp.where(iota(1) == place_ref[0], count.astype(jnp.float32), 0.0)
    tile_ref[...] = jnp.where(iota(0) == 0, counted, fastest)


def swapped(value, index, flip):
    value = pltpu.roll(value, 0, 1, stride=16, stride_axis=0)
    value = jnp.take_along_axis(value, index, axis=0, mode="promise_in_bounds")
    value = pltpu.roll(value, 16, 1, stride=16, stride_axis=0)
    return jnp.take_along_axis(value, flip, axis=0, mode="promise_in_bounds")


def swap_indices():
    row, group = iota(0), iota(1) // 16
    flip = 7 - row
    return (group - flip) & 7, flip


def pack_sides(core, w_ref, xl_ref, xh_ref, yn_ref, yf_ref):
    for layer in range(2):
        for t in range(TS):
            put(xl_ref, layer, t, cells(w_ref, layer, t))
            put(xh_ref, layer, t, cells(w_ref, XS - 2 + layer, t))
    rows = w_ref.reshape(XS * 256, 128)
    high = y_offset(30)
    for layer in range(2):
        for half in range(2):
            for k in range(FIELDS):
                start = half * 2048 + k * 8 + layer
                yn_ref[layer, half, k] = rows[pl.ds(start + (1 - core) * high, 8, stride=256), :]
                yf_ref[layer, half, k] = rows[pl.ds(start + core * high, 8, stride=256), :]


def y_offset(y):
    return (y // 8) * 64 + y % 8


def y_layer(rows, half, k, y):
    return rows[pl.ds(half * 2048 + k * 8 + y_offset(y), 8, stride=256), :]


def assemble_kernel(place_ref, tile_ref, came_ref, own_ref, u_ref, w_ref, xl_ref, xh_ref, yn_ref, yf_ref, slots, sems):
    place = place_ref[0]
    earlier = jnp.where((iota(0) == 0) & (iota(1) < place), tile_ref[...], 0.0)
    surplus = jnp.sum(earlier).astype(jnp.int32) - place * BLK_DEV

    for slot in range(BLK_DEV):
        target = slots.at[slot // 8, :, slot % 8]

        @pl.when(slot < surplus)
        def _():
            source = jnp.clip(BLK_DEV - 1 - surplus + slot, 0, BLK_DEV - 2)
            pltpu.make_async_copy(came_ref.at[source], target, sems.at[slot]).start()

        @pl.when(slot >= surplus)
        def _():
            source = jnp.clip(slot - surplus, 0, BLK_DEV - 1)
            pltpu.make_async_copy(own_ref.at[source], target, sems.at[slot]).start()

    index, flip = swap_indices()
    rows = slots.reshape(2 * CHUNKS * 64, 128)
    for ly in range(2):
        for lz in range(8):
            slot = ly * 8 + lz
            pltpu.make_async_copy(own_ref.at[0], slots.at[ly, :, lz], sems.at[slot]).wait()

        def chunk(c, _):
            state = [swapped(rows[pl.ds((ly * CHUNKS + c) * 64 + k, 8, stride=8), :], index, flip) for k in range(FIELDS)]
            x, t = c // 2, ly * 2 + c % 2
            put(u_ref, x, t, state)
            put(w_ref, x, t, primitive(state))
            return 0

        lax.fori_loop(0, CHUNKS, chunk, 0, unroll=4)
    pack_sides(place % 2, w_ref, xl_ref, xh_ref, yn_ref, yf_ref)


def inner_kernel(w_ref, xz_ref, y_ref, next_ref, prior_ref, flux_ref):
    row = iota(0)
    last, first = row == 7, row == 0

    def ahead(values):
        rolled = [[pltpu.roll(v, 7, 0) for v in w] for w in values]
        rolled.append(rolled[-1])
        return [[jnp.where(last, b, a) for a, b in zip(rolled[t], rolled[t + 1])] for t in range(TS)]

    def behind(values):
        rolled = [[pltpu.roll(v, 1, 0) for v in w] for w in values]
        rolled.insert(0, rolled[0])
        return [[jnp.where(first, a, b) for a, b in zip(rolled[t], rolled[t + 1])] for t in range(TS)]

    def along_y(x, _):
        prims = [cells(w_ref, x, t) for t in range(TS)]
        for t in range(TS):
            put(next_ref, x, t, [pltpu.roll(v, 127, 1) for v in prims[t]])
            put(prior_ref, x, t, [pltpu.roll(v, 1, 1) for v in prims[t]])
        forward = [minus(a, w) for a, w in zip(ahead(prims), prims)]
        backward = behind(forward)
        both = [edges(w, b, f) for w, b, f in zip(prims, backward, forward)]
        right = ahead([lower for _, lower in both])
        flux = [hlle(both[t][0], right[t], 1) for t in range(TS)]
        flux[0] = [jnp.where(first, 0.0, v) for v in flux[0]]
        flux[3] = [jnp.where(row >= 6, 0.0, v) for v in flux[3]]
        rolled = [[pltpu.roll(v, 1, 0) for v in w] for w in flux]
        for t in range(TS):
            if t == 0:
                before = [jnp.where(first, 0.0, v) for v in rolled[0]]
            else:
                before = [jnp.where(first, a, b) for a, b in zip(rolled[t - 1], rolled[t])]
            put(y_ref, x, t, minus(before, flux[t]))
        return 0

    lax.fori_loop(0, XS, along_y, 0, unroll=2)

    def along_z(i, _):
        x, t = i // TS, i % TS
        w = cells(w_ref, x, t)
        upper, lower = edges(w, minus(w, cells(prior_ref, x, t)), minus(cells(next_ref, x, t), w))
        put(flux_ref, x, t, hlle(upper, [pltpu.roll(v, 127, 1) for v in lower], 2))
        return 0

    lax.fori_loop(0, XS * TS, along_z, 0, unroll=8)

    def along_x(pair, _):
        both = (2 * pair, 2 * pair + 1)

        def store(x, t, change=None):
            total = [pltpu.roll(v, 1, 1) - v for v in cells(flux_ref, x, t)]
            put(xz_ref, x, t, total if change is None else plus(total, change))

        start = []
        for t in both:
            w0, w1, w2, w3 = [cells(w_ref, x, t) for x in range(4)]
            d1, d2 = minus(w2, w1), minus(w3, w2)
            upper, _ = edges(w1, minus(w1, w0), d1)
            after, lower = edges(w2, d1, d2)
            flux = hlle(upper, lower, 0)
            store(0, t)
            store(1, t, [-v for v in flux])
            start.append((d2, after, flux))

        def step(x, carry):
            result = []
            for t, (d, upper, flux) in zip(both, carry):
                here, beyond = cells(w_ref, x + 1, t), cells(w_ref, x + 2, t)
                forward = minus(beyond, here)
                after, lower = edges(here, d, forward)
                new = hlle(upper, lower, 0)
                store(x, t, minus(flux, new))
                result.append((forward, after, new))
            return result

        for t, (_, _, flux) in zip(both, lax.fori_loop(2, 14, step, start)):
            store(14, t, flux)
            store(15, t)
        return 0

    lax.fori_loop(0, TS // 2, along_x, 0)


def outer_faces(six, normal):
    ds = [minus(six[i + 1], six[i]) for i in range(len(six) - 1)]
    both = [edges(six[i + 1], ds[i], ds[i + 1]) for i in range(len(six) - 2)]
    return [hlle(both[i][0], both[i + 1][1], normal) for i in range(len(six) - 3)]


def outer(core, w_ref, sides, xc, yc):
    xl_ref, xh_ref, yn_ref, yf_ref = sides

    def column(t, _):
        near = [cells(xl_ref, 0, t), cells(xl_ref, 1, t)] + [cells(w_ref, x, t) for x in range(3)]
        a, b = outer_faces(near, 0)
        put(xc, 0, t, minus(a, b))
        put(xc, 1, t, b)
        far = [cells(w_ref, x, t) for x in range(13, 16)] + [cells(xh_ref, 0, t), cells(xh_ref, 1, t)]
        a, b = outer_faces(far, 0)
        put(xc, 2, t, [-v for v in a])
        put(xc, 3, t, minus(a, b))
        return 0

    lax.fori_loop(0, TS, column, 0)
    rows = w_ref.reshape(XS * 256, 128)
    packed = yc.reshape(XS * 128, 128)
    zero = jnp.zeros((8, 128), jnp.float32)

    def clear(x, _):
        for part in range(2):
            for k in range(FIELDS):
                yc[x, part, k] = zero
        return 0

    lax.fori_loop(0, XS, clear, 0)

    def store(half, part, y, values):
        for k in range(FIELDS):
            packed[pl.ds(half * 1024 + part * 64 + k * 8 + y, 8, stride=128), :] = values[k]

    for half in range(2):
        own = lambda y: [y_layer(rows, half, k, y) for k in range(FIELDS)]
        sent = lambda layer, near: [jnp.where(near, yn_ref[layer, half, k], yf_ref[layer, half, k]) for k in range(FIELDS)]
        a, b = outer_faces([sent(0, core == 1), sent(1, core == 1), own(0), own(1), own(2)], 1)
        store(half, 0, 0, minus(a, b))
        store(half, 0, 1, b)
        a, b = outer_faces([own(29), own(30), own(31), sent(0, core == 0), sent(1, core == 0)], 1)
        store(half, 1, 6, [-v for v in a])
        store(half, 1, 7, minus(a, b))


def changes(inner, xc, yc, x, t, edge):
    xz_ref, y_ref = inner
    total = plus(cells(xz_ref, x, t), cells(y_ref, x, t))
    if t in (0, 3):
        total = plus(total, cells(yc, x, t // 3))
    if edge is not None:
        total = plus(total, cells(xc, edge, t))
    return total


def each_layer(work):
    for edge, x in enumerate((0, 1, XS - 2, XS - 1)):
        work(x, edge)
    lax.fori_loop(2, XS - 2, lambda x, _: (work(x, None), 0)[1], 0)


def step_of(tile_ref):
    return COURANT / jnp.max(jnp.where(iota(0) == 1, tile_ref[...], 0.0))


def first_kernel(place_ref, tile_ref, w_ref, u_ref, txz, ty, xl, xh, yn, yf, s_ref, w2_ref, xl_ref, xh_ref, yn_ref, yf_ref, xc, yc):
    step = step_of(tile_ref)
    core = place_ref[0] % 2
    outer(core, w_ref, (xl, xh, yn, yf), xc, yc)

    def work(x, edge):
        for t in range(TS):
            change = changes((txz, ty), xc, yc, x, t, edge)
            state = cells(u_ref, x, t)
            first = [u + step * c for u, c in zip(state, change)]
            put(s_ref, x, t, [0.5 * (u + f) for u, f in zip(state, first)])
            put(w2_ref, x, t, primitive(first))

    each_layer(work)
    pack_sides(core, w2_ref, xl_ref, xh_ref, yn_ref, yf_ref)


def second_kernel(place_ref, tile_ref, w_ref, s_ref, txz, ty, xl, xh, yn, yf, out_ref, xc, yc, blocks, sems):
    step = 0.5 * step_of(tile_ref)
    outer(place_ref[0] % 2, w_ref, (xl, xh, yn, yf), xc, yc)
    index, flip = swap_indices()
    rows = blocks.reshape(BLK_DEV * CHUNKS * FIELDS, 128)

    def work(x, edge):
        for t in range(TS):
            change = changes((txz, ty), xc, yc, x, t, edge)
            chunk = 2 * x + t % 2
            for k, (s, c) in enumerate(zip(cells(s_ref, x, t), change)):
                start = ((t // 2) * 8 * CHUNKS + chunk) * 8 + k
                rows[pl.ds(start, 8, stride=CHUNKS * 8), :] = swapped(s + step * c, index, flip)

    def part(quarter):
        chunks = pl.ds(quarter * 8, 8)
        return pltpu.make_async_copy(blocks.at[:, chunks], out_ref.at[:, chunks], sems.at[quarter])

    def inside(first, last):
        lax.fori_loop(first, last, lambda x, _: (work(x, None), 0)[1], 0)

    work(0, 0)
    work(1, 1)
    inside(2, 4)
    part(0).start()
    inside(4, 8)
    part(1).start()
    inside(8, 12)
    part(2).start()
    inside(12, 14)
    work(14, 2)
    work(15, 3)
    part(3).start()
    for quarter in range(4):
        part(quarter).wait()


VMEM = pl.BlockSpec(memory_space=pltpu.VMEM)
SMEM = pl.BlockSpec(memory_space=pltpu.SMEM)
ANY = pl.BlockSpec(memory_space=pl.ANY)
HBM = pl.BlockSpec(memory_space=pltpu.HBM)


def shape(dims):
    return pltpu.VMEM(dims, jnp.float32)


def kernel(function, in_specs, outs, scratch, name, flops, limit=LIMIT, out_spec=VMEM):
    single = not isinstance(outs, list)
    return pl.pallas_call(
        function,
        out_shape=jax.ShapeDtypeStruct(outs, jnp.float32) if out_spec is ANY else shape(outs) if single else [shape(dims) for dims in outs],
        in_specs=in_specs,
        out_specs=out_spec if single else [out_spec] * len(outs),
        scratch_shapes=scratch,
        name=name,
        compiler_params=pltpu.CompilerParams(vmem_limit_bytes=limit),
        cost_estimate=pl.CostEstimate(flops=flops, bytes_accessed=6 << 20, transcendentals=0),
    )


def shifted(value, axis, by):
    count = lax.axis_size(axis)
    return lax.ppermute(value, axis, [(i, (i + by) % count) for i in range(count)])


def exchanged(xl, xh, yn, yf):
    count = lax.axis_size("dev")
    near = [(i, i ^ 1) for i in range(count)]
    far = [(i, (i + 1) % count if i % 2 else (i - 1) % count) for i in range(count)]
    return shifted(xh, "group", 1), shifted(xl, "group", -1), lax.ppermute(yn, "dev", near), lax.ppermute(yf, "dev", far)


def body(blocks_in, counts):
    devices = lax.axis_size(AXES)
    place = lax.axis_index(AXES).astype(jnp.int32).reshape(1)
    tiles = lambda value: value.reshape(value.shape[0], FIELDS, CHUNKS, 128).swapaxes(1, 2)
    own = tiles(blocks_in)
    passed = (BLK_DEV - 1, CHUNKS, FIELDS, 128)
    there = pltpu.with_memory_space_constraint(own, pltpu.HBM)
    outgoing = kernel(outgoing_kernel, [SMEM, HBM], passed, [pltpu.SemaphoreType.DMA((BLK_DEV - 1,))], "outgoing", 1 << 10)(
        counts, there
    )
    came = lax.ppermute(outgoing, AXES, [(i, i + 1) for i in range(devices - 1)])
    tile = kernel(
        speed_kernel,
        [SMEM, SMEM, HBM],
        (8, 128),
        [
            pltpu.VMEM((blocks_in.shape[0], CHUNKS, FIELDS, 128), jnp.float32),
            pltpu.SemaphoreType.DMA((pl.cdiv(blocks_in.shape[0], 4),)),
        ],
        "signal_speed",
        1 << 20,
    )(counts, place, there)
    tile = jnp.maximum(tile, lax.ppermute(tile, AXES, [(i, i ^ 1) for i in range(devices)]))
    tile, own = lax.optimization_barrier((tile, own))
    for masks in ROUNDS:
        tile = jnp.maximum(tile, lax.ppermute(tile, AXES, [(i, i ^ masks[i % 2]) for i in range(devices)]))
    tile = jnp.maximum(tile, lax.ppermute(tile, AXES, [(i, i ^ 1) for i in range(devices)]))
    sides = [XFACE, XFACE, YFACE, YFACE]
    u, w, *faces = kernel(
        assemble_kernel,
        [SMEM, VMEM, ANY, ANY],
        [GRID, GRID] + sides,
        [pltpu.VMEM((2, CHUNKS, 8, FIELDS, 128), jnp.float32), pltpu.SemaphoreType.DMA((BLK_DEV,))],
        "assemble",
        1 << 20,
    )(place, tile, came, own)
    corrections = [pltpu.VMEM((4, TS, FIELDS, 8, 128), jnp.float32), pltpu.VMEM((XS, 2, FIELDS, 8, 128), jnp.float32)]
    inner = kernel(inner_kernel, [VMEM], [GRID] * 2, [pltpu.VMEM(GRID, jnp.float32)] * 3, "inner_fluxes", 40 << 20)
    specs = [SMEM] + [VMEM] * 9
    ghosts = exchanged(*faces)
    s, w2, *faces = kernel(first_kernel, specs, [GRID, GRID] + sides, corrections, "first_stage", 1 << 20)(
        place, tile, w, u, *inner(w), *ghosts
    )
    ghosts = exchanged(*faces)
    result = (BLK_DEV, CHUNKS, FIELDS, 128)
    buffers = corrections + [pltpu.VMEM(result, jnp.float32), pltpu.SemaphoreType.DMA((4,))]
    out = kernel(second_kernel, specs, result, buffers, "second_stage", 1 << 20, out_spec=ANY)(
        place, tile, w2, s, *inner(w2), *ghosts
    )
    return out.swapaxes(1, 2).reshape(BLK_DEV, FIELDS, BS * BS * BS)


def solution(mesh):
    in_specs = (P(AXES, None, None), P(AXES))
    out_specs = P(AXES, None, None)
    return jax.shard_map(body, mesh=mesh, in_specs=in_specs, out_specs=out_specs, check_vma=False)
```

```python
import functools

import jax
import jax.numpy as jnp
from jax import lax
from jax.experimental import pallas as pl
from jax.experimental.pallas import tpu as pltpu
from jax.sharding import PartitionSpec as P

BS = 16
BLK_DEV = 16
FIELDS = 8
XS = 16
TS = 4
CHUNKS = 32
AXES = ("group", "dev")
ROUNDS = ((2, 32), (6, 96), (8, 32), (24, 96), (32, 32), (96, 96))

GAMMA = 5.0 / 3.0
COURANT = 0.25
DENSITY_FLOOR = 0.05
PRESSURE_FLOOR = 0.05
TINY = 1e-37

GRID = (XS, TS, FIELDS, 8, 128)
XFACE = (2, TS, FIELDS, 8, 128)
YFACE = (2, 2, FIELDS, 8, 128)
LIMIT = 24 << 20


def iota(axis):
    return lax.broadcasted_iota(jnp.int32, (8, 128), axis)


def root(value):
    return value * lax.rsqrt(value)


def primitive(state):
    density = jnp.maximum(state[0], DENSITY_FLOOR)
    inverse = 1.0 / density
    velocity = [state[k] * inverse for k in (1, 2, 3)]
    magnetic = state[5:8]
    kinetic = 0.5 * density * (velocity[0] * velocity[0] + velocity[1] * velocity[1] + velocity[2] * velocity[2])
    field = 0.5 * (magnetic[0] * magnetic[0] + magnetic[1] * magnetic[1] + magnetic[2] * magnetic[2])
    pressure = jnp.maximum((GAMMA - 1.0) * (state[4] - kinetic - field), PRESSURE_FLOOR)
    return [density] + velocity + [pressure] + list(magnetic)


def fast_speed(prims, normal, inverse, half):
    magnetic = prims[5:8]
    along = magnetic[normal] * magnetic[normal] * inverse
    sound = (0.5 * GAMMA * prims[4]) * inverse
    total = sound + half * inverse
    inner = jnp.maximum(total * total - (2.0 * sound) * along, TINY)
    return root(total + root(inner))


def half_square(field):
    return 0.5 * (field[0] * field[0] + field[1] * field[1] + field[2] * field[2])


def side(prims, normal):
    density, pressure = prims[0], prims[4]
    velocity, magnetic = prims[1:4], prims[5:8]
    half = half_square(magnetic)
    fast = fast_speed(prims, normal, 1.0 / density, half)
    total = pressure + half
    motion = velocity[0] * velocity[0] + velocity[1] * velocity[1] + velocity[2] * velocity[2]
    energy = total + 0.5 * (pressure + density * motion)
    cross = velocity[0] * magnetic[0] + velocity[1] * magnetic[1] + velocity[2] * magnetic[2]
    return fast, total, energy, cross


def weighed(prims, normal, weight, other, total, energy, cross):
    density = prims[0]
    velocity, magnetic = prims[1:4], prims[5:8]
    carried = weight * (velocity[normal] - other)
    bent = weight * magnetic[normal]
    mass = carried * density
    push = weight * total
    momentum = [mass * velocity[k] - bent * magnetic[k] for k in range(3)]
    momentum[normal] = momentum[normal] + push
    power = carried * energy + push * velocity[normal] - bent * cross
    induced = [carried * magnetic[k] - bent * velocity[k] for k in range(3)]
    induced[normal] = other * bent
    return [mass] + momentum + [power] + induced


def hlle(left, right, normal):
    fast_l, total_l, energy_l, cross_l = side(left, normal)
    fast_r, total_r, energy_r, cross_r = side(right, normal)
    speed_l, speed_r = left[1 + normal], right[1 + normal]
    upper = jnp.maximum(jnp.maximum(speed_r + fast_r, speed_l + fast_l), 0.0)
    lower = jnp.minimum(jnp.minimum(speed_l - fast_l, speed_r - fast_r), 0.0)
    weight = upper * (1.0 / (upper - lower))
    part_l = weighed(left, normal, weight, lower, total_l, energy_l, cross_l)
    part_r = weighed(right, normal, 1.0 - weight, upper, total_r, energy_r, cross_r)
    flux = [a + b for a, b in zip(part_l, part_r)]
    flux[5 + normal] = -flux[5 + normal]
    return flux


def minus(first, second):
    return [a - b for a, b in zip(first, second)]


def plus(first, second):
    return [a + b for a, b in zip(first, second)]


def edges(prims, backward, forward):
    upper, lower = [], []
    for w, a, b in zip(prims, backward, forward):
        half = 0.5 * jnp.maximum(jnp.minimum(a, b), jnp.minimum(jnp.maximum(a, b), 0.0))
        upper.append(w + half)
        lower.append(w - half)
    return upper, lower


def cells(ref, x, t):
    return [ref[x, t, k] for k in range(FIELDS)]


def put(ref, x, t, values):
    for k in range(FIELDS):
        ref[x, t, k] = values[k]


def outgoing_kernel(count_ref, blocks_ref, out_ref, sems):
    count, places = count_ref[0], BLK_DEV - 1

    def each(work):
        for place in range(places):
            slot = count - places + place

            @pl.when(slot >= 0)
            def _():
                source = jnp.clip(slot, 0, blocks_ref.shape[0] - 1)
                work(pltpu.make_async_copy(blocks_ref.at[source], out_ref.at[place], sems.at[place]))

    each(lambda copy: copy.start())
    each(lambda copy: copy.wait())


def speed_kernel(count_ref, place_ref, blocks_ref, tile_ref, slots, sems):
    count = count_ref[0]
    group = 4
    groups = pl.cdiv(blocks_ref.shape[0], group)

    def incoming(index, work):
        size = min(group, blocks_ref.shape[0] - index * group)
        part = pl.ds(index * group, size)

        @pl.when(index * group < count)
        def _():
            work(pltpu.make_async_copy(blocks_ref.at[part], slots.at[part], sems.at[index]))

    for index in range(groups):
        incoming(index, lambda copy: copy.start())

    rows = slots.reshape(slots.shape[0] * CHUNKS * FIELDS, 128)

    def speeds(start, tops):
        prims = primitive([rows[pl.ds(start + k, 8, stride=8), :] for k in range(FIELDS)])
        half = half_square(prims[5:8])
        inverse = 1.0 / prims[0]
        for normal in range(3):
            speed = jnp.abs(prims[1 + normal]) + fast_speed(prims, normal, inverse, half)
            tops[normal] = jnp.maximum(tops[normal], speed)

    def several(index, tops):
        for which in range(groups):
            @pl.when(index == which)
            def _():
                incoming(which, lambda copy: copy.wait())
        tops = list(tops)
        for which in range(group):
            slot = jnp.minimum(index * group + which, count - 1)
            for part in range(4):
                speeds(slot * (CHUNKS * FIELDS) + part * 64, tops)
        return tuple(tops)

    tops = lax.fori_loop(0, pl.cdiv(count, group), several, (jnp.zeros((8, 128), jnp.float32),) * 3)
    fastest = jnp.max(jnp.maximum(jnp.maximum(tops[0], tops[1]), tops[2]))
    counted = jnp.where(iota(1) == place_ref[0], count.astype(jnp.float32), 0.0)
    tile_ref[...] = jnp.where(iota(0) == 0, counted, fastest)


def swapped(value, index, flip):
    value = pltpu.roll(value, 0, 1, stride=16, stride_axis=0)
    value = jnp.take_along_axis(value, index, axis=0, mode="promise_in_bounds")
    value = pltpu.roll(value, 16, 1, stride=16, stride_axis=0)
    return jnp.take_along_axis(value, flip, axis=0, mode="promise_in_bounds")


def swap_indices():
    row, group = iota(0), iota(1) // 16
    flip = 7 - row
    return (group - flip) & 7, flip


def pack_sides(core, w_ref, xl_ref, xh_ref, yn_ref, yf_ref):
    for layer in range(2):
        for t in range(TS):
            put(xl_ref, layer, t, cells(w_ref, layer, t))
            put(xh_ref, layer, t, cells(w_ref, XS - 2 + layer, t))
    rows = w_ref.reshape(XS * 256, 128)
    high = y_offset(30)
    for layer in range(2):
        for half in range(2):
            for k in range(FIELDS):
                start = half * 2048 + k * 8 + layer
                yn_ref[layer, half, k] = rows[pl.ds(start + (1 - core) * high, 8, stride=256), :]
                yf_ref[layer, half, k] = rows[pl.ds(start + core * high, 8, stride=256), :]


def y_offset(y):
    return (y // 8) * 64 + y % 8


def y_layer(rows, half, k, y):
    return rows[pl.ds(half * 2048 + k * 8 + y_offset(y), 8, stride=256), :]


def assemble_kernel(place_ref, tile_ref, came_ref, own_ref, u_ref, w_ref, xl_ref, xh_ref, yn_ref, yf_ref, slots, sems):
    place = place_ref[0]
    earlier = jnp.where((iota(0) == 0) & (iota(1) < place), tile_ref[...], 0.0)
    surplus = jnp.sum(earlier).astype(jnp.int32) - place * BLK_DEV

    for slot in range(BLK_DEV):
        target = slots.at[slot // 8, :, slot % 8]

        @pl.when(slot < surplus)
        def _():
            source = jnp.clip(BLK_DEV - 1 - surplus + slot, 0, BLK_DEV - 2)
            pltpu.make_async_copy(came_ref.at[source], target, sems.at[slot]).start()

        @pl.when(slot >= surplus)
        def _():
            source = jnp.clip(slot - surplus, 0, BLK_DEV - 1)
            pltpu.make_async_copy(own_ref.at[source], target, sems.at[slot]).start()

    index, flip = swap_indices()
    rows = slots.reshape(2 * CHUNKS * 64, 128)
    for ly in range(2):
        for lz in range(8):
            slot = ly * 8 + lz
            pltpu.make_async_copy(own_ref.at[0], slots.at[ly, :, lz], sems.at[slot]).wait()

        def chunk(c, _):
            state = [swapped(rows[pl.ds((ly * CHUNKS + c) * 64 + k, 8, stride=8), :], index, flip) for k in range(FIELDS)]
            x, t = c // 2, ly * 2 + c % 2
            put(u_ref, x, t, state)
            put(w_ref, x, t, primitive(state))
            return 0

        lax.fori_loop(0, CHUNKS, chunk, 0, unroll=16)
    pack_sides(place % 2, w_ref, xl_ref, xh_ref, yn_ref, yf_ref)


def inner_kernel(w_ref, xz_ref, y_ref, next_ref, prior_ref, flux_ref):
    row = iota(0)
    last, first = row == 7, row == 0

    def ahead(values):
        rolled = [[pltpu.roll(v, 7, 0) for v in w] for w in values]
        rolled.append(rolled[-1])
        return [[jnp.where(last, b, a) for a, b in zip(rolled[t], rolled[t + 1])] for t in range(TS)]

    def behind(values):
        rolled = [[pltpu.roll(v, 1, 0) for v in w] for w in values]
        rolled.insert(0, rolled[0])
        return [[jnp.where(first, a, b) for a, b in zip(rolled[t], rolled[t + 1])] for t in range(TS)]

    def along_y(x, _):
        prims = [cells(w_ref, x, t) for t in range(TS)]
        for t in range(TS):
            put(next_ref, x, t, [pltpu.roll(v, 127, 1) for v in prims[t]])
            put(prior_ref, x, t, [pltpu.roll(v, 1, 1) for v in prims[t]])
        forward = [minus(a, w) for a, w in zip(ahead(prims), prims)]
        backward = behind(forward)
        both = [edges(w, b, f) for w, b, f in zip(prims, backward, forward)]
        right = ahead([lower for _, lower in both])
        flux = [hlle(both[t][0], right[t], 1) for t in range(TS)]
        flux[0] = [jnp.where(first, 0.0, v) for v in flux[0]]
        flux[3] = [jnp.where(row >= 6, 0.0, v) for v in flux[3]]
        rolled = [[pltpu.roll(v, 1, 0) for v in w] for w in flux]
        for t in range(TS):
            if t == 0:
                before = [jnp.where(first, 0.0, v) for v in rolled[0]]
            else:
                before = [jnp.where(first, a, b) for a, b in zip(rolled[t - 1], rolled[t])]
            put(y_ref, x, t, minus(before, flux[t]))
        return 0

    lax.fori_loop(0, XS, along_y, 0, unroll=2)

    def along_z(i, _):
        x, t = i // TS, i % TS
        w = cells(w_ref, x, t)
        upper, lower = edges(w, minus(w, cells(prior_ref, x, t)), minus(cells(next_ref, x, t), w))
        put(flux_ref, x, t, hlle(upper, [pltpu.roll(v, 127, 1) for v in lower], 2))
        return 0

    lax.fori_loop(0, XS * TS, along_z, 0, unroll=8)

    def along_x(pair, _):
        both = (2 * pair, 2 * pair + 1)

        def store(x, t, change=None):
            total = [pltpu.roll(v, 1, 1) - v for v in cells(flux_ref, x, t)]
            put(xz_ref, x, t, total if change is None else plus(total, change))

        start = []
        for t in both:
            w0, w1, w2, w3 = [cells(w_ref, x, t) for x in range(4)]
            d1, d2 = minus(w2, w1), minus(w3, w2)
            upper, _ = edges(w1, minus(w1, w0), d1)
            after, lower = edges(w2, d1, d2)
            flux = hlle(upper, lower, 0)
            store(0, t)
            store(1, t, [-v for v in flux])
            start.append((d2, after, flux))

        def step(x, carry):
            result = []
            for t, (d, upper, flux) in zip(both, carry):
                here, beyond = cells(w_ref, x + 1, t), cells(w_ref, x + 2, t)
                forward = minus(beyond, here)
                after, lower = edges(here, d, forward)
                new = hlle(upper, lower, 0)
                store(x, t, minus(flux, new))
                result.append((forward, after, new))
            return result

        for t, (_, _, flux) in zip(both, lax.fori_loop(2, 14, step, start, unroll=3)):
            store(14, t, flux)
            store(15, t)
        return 0

    lax.fori_loop(0, TS // 2, along_x, 0)


def outer_faces(six, normal):
    ds = [minus(six[i + 1], six[i]) for i in range(len(six) - 1)]
    both = [edges(six[i + 1], ds[i], ds[i + 1]) for i in range(len(six) - 2)]
    return [hlle(both[i][0], both[i + 1][1], normal) for i in range(len(six) - 3)]


def outer(core, w_ref, sides, xc, yc):
    xl_ref, xh_ref, yn_ref, yf_ref = sides

    def column(t, _):
        near = [cells(xl_ref, 0, t), cells(xl_ref, 1, t)] + [cells(w_ref, x, t) for x in range(3)]
        a, b = outer_faces(near, 0)
        put(xc, 0, t, minus(a, b))
        put(xc, 1, t, b)
        far = [cells(w_ref, x, t) for x in range(13, 16)] + [cells(xh_ref, 0, t), cells(xh_ref, 1, t)]
        a, b = outer_faces(far, 0)
        put(xc, 2, t, [-v for v in a])
        put(xc, 3, t, minus(a, b))
        return 0

    lax.fori_loop(0, TS, column, 0, unroll=4)
    rows = w_ref.reshape(XS * 256, 128)
    packed = yc.reshape(XS * 128, 128)
    zero = jnp.zeros((8, 128), jnp.float32)

    def clear(x, _):
        for part in range(2):
            for k in range(FIELDS):
                yc[x, part, k] = zero
        return 0

    lax.fori_loop(0, XS, clear, 0)

    def store(half, part, y, values):
        for k in range(FIELDS):
            packed[pl.ds(half * 1024 + part * 64 + k * 8 + y, 8, stride=128), :] = values[k]

    for half in range(2):
        own = lambda y: [y_layer(rows, half, k, y) for k in range(FIELDS)]
        sent = lambda layer, near: [jnp.where(near, yn_ref[layer, half, k], yf_ref[layer, half, k]) for k in range(FIELDS)]
        a, b = outer_faces([sent(0, core == 1), sent(1, core == 1), own(0), own(1), own(2)], 1)
        store(half, 0, 0, minus(a, b))
        store(half, 0, 1, b)
        a, b = outer_faces([own(29), own(30), own(31), sent(0, core == 0), sent(1, core == 0)], 1)
        store(half, 1, 6, [-v for v in a])
        store(half, 1, 7, minus(a, b))


def changes(inner, xc, yc, x, t, edge):
    xz_ref, y_ref = inner
    total = plus(cells(xz_ref, x, t), cells(y_ref, x, t))
    if t in (0, 3):
        total = plus(total, cells(yc, x, t // 3))
    if edge is not None:
        total = plus(total, cells(xc, edge, t))
    return total


def each_layer(work):
    for edge, x in enumerate((0, 1, XS - 2, XS - 1)):
        work(x, edge)
    lax.fori_loop(2, XS - 2, lambda x, _: (work(x, None), 0)[1], 0, unroll=4)


def step_of(tile_ref):
    return COURANT / jnp.max(jnp.where(iota(0) == 1, tile_ref[...], 0.0))


def first_kernel(place_ref, tile_ref, w_ref, u_ref, txz, ty, xl, xh, yn, yf, s_ref, w2_ref, xl_ref, xh_ref, yn_ref, yf_ref, xc, yc):
    step = step_of(tile_ref)
    core = place_ref[0] % 2
    outer(core, w_ref, (xl, xh, yn, yf), xc, yc)

    def work(x, edge):
        for t in range(TS):
            change = changes((txz, ty), xc, yc, x, t, edge)
            state = cells(u_ref, x, t)
            first = [u + step * c for u, c in zip(state, change)]
            put(s_ref, x, t, [0.5 * (u + f) for u, f in zip(state, first)])
            put(w2_ref, x, t, primitive(first))

    each_layer(work)
    pack_sides(core, w2_ref, xl_ref, xh_ref, yn_ref, yf_ref)


def second_kernel(place_ref, tile_ref, w_ref, s_ref, txz, ty, xl, xh, yn, yf, out_ref, xc, yc, blocks, sems):
    step = 0.5 * step_of(tile_ref)
    outer(place_ref[0] % 2, w_ref, (xl, xh, yn, yf), xc, yc)
    index, flip = swap_indices()
    rows = blocks.reshape(BLK_DEV * CHUNKS * FIELDS, 128)

    def work(x, edge):
        for t in range(TS):
            change = changes((txz, ty), xc, yc, x, t, edge)
            chunk = 2 * x + t % 2
            for k, (s, c) in enumerate(zip(cells(s_ref, x, t), change)):
                start = ((t // 2) * 8 * CHUNKS + chunk) * 8 + k
                rows[pl.ds(start, 8, stride=CHUNKS * 8), :] = swapped(s + step * c, index, flip)

    def part(quarter):
        chunks = pl.ds(quarter * 8, 8)
        return pltpu.make_async_copy(blocks.at[:, chunks], out_ref.at[:, chunks], sems.at[quarter])

    def pairs(first, last):
        lax.fori_loop(first, last, lambda x, _: (work(x, None), 0)[1], 0, unroll=min(4, last - first))

    work(0, 0)
    work(1, 1)
    pairs(2, 4)
    part(0).start()
    pairs(4, 8)
    part(1).start()
    pairs(8, 12)
    part(2).start()
    pairs(12, 14)
    work(14, 2)
    work(15, 3)
    part(3).start()
    for quarter in range(4):
        part(quarter).wait()


VMEM = pl.BlockSpec(memory_space=pltpu.VMEM)
SMEM = pl.BlockSpec(memory_space=pltpu.SMEM)
ANY = pl.BlockSpec(memory_space=pl.ANY)
HBM = pl.BlockSpec(memory_space=pltpu.HBM)


def shape(dims):
    return pltpu.VMEM(dims, jnp.float32)


def kernel(function, in_specs, outs, scratch, name, flops, limit=LIMIT, out_spec=VMEM):
    single = not isinstance(outs, list)
    return pl.pallas_call(
        function,
        out_shape=jax.ShapeDtypeStruct(outs, jnp.float32) if out_spec is ANY else shape(outs) if single else [shape(dims) for dims in outs],
        in_specs=in_specs,
        out_specs=out_spec if single else [out_spec] * len(outs),
        scratch_shapes=scratch,
        name=name,
        compiler_params=pltpu.CompilerParams(vmem_limit_bytes=limit),
        cost_estimate=pl.CostEstimate(flops=flops, bytes_accessed=6 << 20, transcendentals=0),
    )


def shifted(value, axis, by):
    count = lax.axis_size(axis)
    return lax.ppermute(value, axis, [(i, (i + by) % count) for i in range(count)])


def exchanged(xl, xh, yn, yf):
    count = lax.axis_size("dev")
    near = [(i, i ^ 1) for i in range(count)]
    far = [(i, (i + 1) % count if i % 2 else (i - 1) % count) for i in range(count)]
    return shifted(xh, "group", 1), shifted(xl, "group", -1), lax.ppermute(yn, "dev", near), lax.ppermute(yf, "dev", far)


def body(blocks_in, counts):
    devices = lax.axis_size(AXES)
    place = lax.axis_index(AXES).astype(jnp.int32).reshape(1)
    tiles = lambda value: value.reshape(value.shape[0], FIELDS, CHUNKS, 128).swapaxes(1, 2)
    own = tiles(blocks_in)
    passed = (BLK_DEV - 1, CHUNKS, FIELDS, 128)
    there = pltpu.with_memory_space_constraint(own, pltpu.HBM)
    outgoing = kernel(outgoing_kernel, [SMEM, HBM], passed, [pltpu.SemaphoreType.DMA((BLK_DEV - 1,))], "outgoing", 1 << 10)(
        counts, there
    )
    came = lax.ppermute(outgoing, AXES, [(i, i + 1) for i in range(devices - 1)])
    tile = kernel(
        speed_kernel,
        [SMEM, SMEM, HBM],
        (8, 128),
        [
            pltpu.VMEM((blocks_in.shape[0], CHUNKS, FIELDS, 128), jnp.float32),
            pltpu.SemaphoreType.DMA((pl.cdiv(blocks_in.shape[0], 4),)),
        ],
        "signal_speed",
        1 << 20,
    )(counts, place, there)
    tile = jnp.maximum(tile, lax.ppermute(tile, AXES, [(i, i ^ 1) for i in range(devices)]))
    for masks in ROUNDS:
        tile = jnp.maximum(tile, lax.ppermute(tile, AXES, [(i, i ^ masks[i % 2]) for i in range(devices)]))
    tile = jnp.maximum(tile, lax.ppermute(tile, AXES, [(i, i ^ 1) for i in range(devices)]))
    sides = [XFACE, XFACE, YFACE, YFACE]
    u, w, *faces = kernel(
        assemble_kernel,
        [SMEM, VMEM, ANY, ANY],
        [GRID, GRID] + sides,
        [pltpu.VMEM((2, CHUNKS, 8, FIELDS, 128), jnp.float32), pltpu.SemaphoreType.DMA((BLK_DEV,))],
        "assemble",
        1 << 20,
    )(place, tile, pltpu.with_memory_space_constraint(came, pltpu.HBM), there)
    corrections = [pltpu.VMEM((4, TS, FIELDS, 8, 128), jnp.float32), pltpu.VMEM((XS, 2, FIELDS, 8, 128), jnp.float32)]
    inner = kernel(inner_kernel, [VMEM], [GRID] * 2, [pltpu.VMEM(GRID, jnp.float32)] * 3, "inner_fluxes", 40 << 20)
    specs = [SMEM] + [VMEM] * 9
    ghosts = exchanged(*faces)
    s, w2, *faces = kernel(first_kernel, specs, [GRID, GRID] + sides, corrections, "first_stage", 1 << 20)(
        place, tile, w, u, *inner(w), *ghosts
    )
    ghosts = exchanged(*faces)
    result = (BLK_DEV, CHUNKS, FIELDS, 128)
    buffers = corrections + [pltpu.VMEM(result, jnp.float32), pltpu.SemaphoreType.DMA((4,))]
    out = kernel(second_kernel, specs, result, buffers, "second_stage", 1 << 20, out_spec=ANY)(
        place, tile, w2, s, *inner(w2), *ghosts
    )
    return out.swapaxes(1, 2).reshape(BLK_DEV, FIELDS, BS * BS * BS)


def solution(mesh):
    in_specs = (P(AXES, None, None), P(AXES))
    out_specs = P(AXES, None, None)
    return jax.shard_map(body, mesh=mesh, in_specs=in_specs, out_specs=out_specs, check_vma=False)
```

```python
import functools

import jax
import jax.numpy as jnp
from jax import lax
from jax.experimental import pallas as pl
from jax.experimental.pallas import tpu as pltpu
from jax.sharding import PartitionSpec as P

BS = 16
BLK_DEV = 16
FIELDS = 8
XS = 16
TS = 4
CHUNKS = 32
AXES = ("group", "dev")
ROUNDS = ((2, 32), (6, 96), (8, 32), (24, 96), (32, 32), (96, 96))

GAMMA = 5.0 / 3.0
COURANT = 0.25
DENSITY_FLOOR = 0.05
PRESSURE_FLOOR = 0.05
TINY = 1e-37

GRID = (XS, TS, FIELDS, 8, 128)
XFACE = (2, TS, FIELDS, 8, 128)
YFACE = (2, 2, FIELDS, 8, 128)
LIMIT = 24 << 20


def iota(axis):
    return lax.broadcasted_iota(jnp.int32, (8, 128), axis)


def root(value):
    return value * lax.rsqrt(value)


def primitive(state):
    density = jnp.maximum(state[0], DENSITY_FLOOR)
    inverse = 1.0 / density
    velocity = [state[k] * inverse for k in (1, 2, 3)]
    magnetic = state[5:8]
    kinetic = 0.5 * density * (velocity[0] * velocity[0] + velocity[1] * velocity[1] + velocity[2] * velocity[2])
    field = 0.5 * (magnetic[0] * magnetic[0] + magnetic[1] * magnetic[1] + magnetic[2] * magnetic[2])
    pressure = jnp.maximum((GAMMA - 1.0) * (state[4] - kinetic - field), PRESSURE_FLOOR)
    return [density] + velocity + [pressure] + list(magnetic)


def fast_speed(prims, normal, inverse, half):
    magnetic = prims[5:8]
    along = magnetic[normal] * magnetic[normal] * inverse
    sound = (0.5 * GAMMA * prims[4]) * inverse
    total = sound + half * inverse
    inner = jnp.maximum(total * total - (2.0 * sound) * along, TINY)
    return root(total + root(inner))


def half_square(field):
    return 0.5 * (field[0] * field[0] + field[1] * field[1] + field[2] * field[2])


def side(prims, normal):
    density, pressure = prims[0], prims[4]
    velocity, magnetic = prims[1:4], prims[5:8]
    half = half_square(magnetic)
    fast = fast_speed(prims, normal, 1.0 / density, half)
    total = pressure + half
    motion = velocity[0] * velocity[0] + velocity[1] * velocity[1] + velocity[2] * velocity[2]
    energy = total + 0.5 * (pressure + density * motion)
    cross = velocity[0] * magnetic[0] + velocity[1] * magnetic[1] + velocity[2] * magnetic[2]
    return fast, total, energy, cross


def weighed(prims, normal, weight, other, total, energy, cross):
    density = prims[0]
    velocity, magnetic = prims[1:4], prims[5:8]
    carried = weight * (velocity[normal] - other)
    bent = weight * magnetic[normal]
    mass = carried * density
    push = weight * total
    momentum = [mass * velocity[k] - bent * magnetic[k] for k in range(3)]
    momentum[normal] = momentum[normal] + push
    power = carried * energy + push * velocity[normal] - bent * cross
    induced = [carried * magnetic[k] - bent * velocity[k] for k in range(3)]
    induced[normal] = other * bent
    return [mass] + momentum + [power] + induced


def hlle(left, right, normal):
    fast_l, total_l, energy_l, cross_l = side(left, normal)
    fast_r, total_r, energy_r, cross_r = side(right, normal)
    speed_l, speed_r = left[1 + normal], right[1 + normal]
    upper = jnp.maximum(jnp.maximum(speed_r + fast_r, speed_l + fast_l), 0.0)
    lower = jnp.minimum(jnp.minimum(speed_l - fast_l, speed_r - fast_r), 0.0)
    weight = upper * (1.0 / (upper - lower))
    part_l = weighed(left, normal, weight, lower, total_l, energy_l, cross_l)
    part_r = weighed(right, normal, 1.0 - weight, upper, total_r, energy_r, cross_r)
    flux = [a + b for a, b in zip(part_l, part_r)]
    flux[5 + normal] = -flux[5 + normal]
    return flux


def minus(first, second):
    return [a - b for a, b in zip(first, second)]


def plus(first, second):
    return [a + b for a, b in zip(first, second)]


def edges(prims, backward, forward):
    upper, lower = [], []
    for w, a, b in zip(prims, backward, forward):
        half = jnp.maximum(jnp.minimum(a, b), jnp.minimum(jnp.maximum(a, b), 0.0))
        upper.append(w + half)
        lower.append(w - half)
    return upper, lower


def cells(ref, x, t):
    return [ref[x, t, k] for k in range(FIELDS)]


def put(ref, x, t, values):
    for k in range(FIELDS):
        ref[x, t, k] = values[k]


def outgoing_kernel(count_ref, blocks_ref, out_ref, sems):
    count, places = count_ref[0], BLK_DEV - 1

    def each(work):
        for place in range(places):
            slot = count - places + place

            @pl.when(slot >= 0)
            def _():
                source = jnp.clip(slot, 0, blocks_ref.shape[0] - 1)
                work(pltpu.make_async_copy(blocks_ref.at[source], out_ref.at[place], sems.at[place]))

    each(lambda copy: copy.start())
    each(lambda copy: copy.wait())


def speed_kernel(count_ref, place_ref, blocks_ref, tile_ref, slots, sems):
    count = count_ref[0]
    group = 4
    groups = pl.cdiv(blocks_ref.shape[0], group)

    def incoming(index, work):
        size = min(group, blocks_ref.shape[0] - index * group)
        part = pl.ds(index * group, size)

        @pl.when(index * group < count)
        def _():
            work(pltpu.make_async_copy(blocks_ref.at[part], slots.at[part], sems.at[index]))

    for index in range(groups):
        incoming(index, lambda copy: copy.start())

    rows = slots.reshape(slots.shape[0] * CHUNKS * FIELDS, 128)

    def speeds(start, tops):
        prims = primitive([rows[pl.ds(start + k, 8, stride=8), :] for k in range(FIELDS)])
        half = half_square(prims[5:8])
        inverse = 1.0 / prims[0]
        for normal in range(3):
            speed = jnp.abs(prims[1 + normal]) + fast_speed(prims, normal, inverse, half)
            tops[normal] = jnp.maximum(tops[normal], speed)

    def several(index, tops):
        for which in range(groups):
            @pl.when(index == which)
            def _():
                incoming(which, lambda copy: copy.wait())
        tops = list(tops)
        for which in range(group):
            slot = jnp.minimum(index * group + which, count - 1)
            for part in range(4):
                speeds(slot * (CHUNKS * FIELDS) + part * 64, tops)
        return tuple(tops)

    tops = lax.fori_loop(0, pl.cdiv(count, group), several, (jnp.zeros((8, 128), jnp.float32),) * 3)
    fastest = jnp.max(jnp.maximum(jnp.maximum(tops[0], tops[1]), tops[2]))
    counted = jnp.where(iota(1) == place_ref[0], count.astype(jnp.float32), 0.0)
    tile_ref[...] = jnp.where(iota(0) == 0, counted, fastest)


def swapped(value, index, flip):
    value = pltpu.roll(value, 0, 1, stride=16, stride_axis=0)
    value = jnp.take_along_axis(value, index, axis=0, mode="promise_in_bounds")
    value = pltpu.roll(value, 16, 1, stride=16, stride_axis=0)
    return jnp.take_along_axis(value, flip, axis=0, mode="promise_in_bounds")


def swap_indices():
    row, group = iota(0), iota(1) // 16
    flip = 7 - row
    return (group - flip) & 7, flip


def pack_sides(core, w_ref, xl_ref, xh_ref, yn_ref, yf_ref):
    for layer in range(2):
        for t in range(TS):
            put(xl_ref, layer, t, cells(w_ref, layer, t))
            put(xh_ref, layer, t, cells(w_ref, XS - 2 + layer, t))
    rows = w_ref.reshape(XS * 256, 128)
    high = y_offset(30)
    for layer in range(2):
        for half in range(2):
            for k in range(FIELDS):
                start = half * 2048 + k * 8 + layer
                yn_ref[layer, half, k] = rows[pl.ds(start + (1 - core) * high, 8, stride=256), :]
                yf_ref[layer, half, k] = rows[pl.ds(start + core * high, 8, stride=256), :]


def y_offset(y):
    return (y // 8) * 64 + y % 8


def y_layer(rows, half, k, y):
    return rows[pl.ds(half * 2048 + k * 8 + y_offset(y), 8, stride=256), :]


def assemble_kernel(place_ref, tile_ref, came_ref, own_ref, u_ref, w_ref, xl_ref, xh_ref, yn_ref, yf_ref, slots, sems):
    place = place_ref[0]
    earlier = jnp.where((iota(0) == 0) & (iota(1) < place), tile_ref[...], 0.0)
    surplus = jnp.sum(earlier).astype(jnp.int32) - place * BLK_DEV

    for slot in range(BLK_DEV):
        target = slots.at[slot // 8, :, slot % 8]

        @pl.when(slot < surplus)
        def _():
            source = jnp.clip(BLK_DEV - 1 - surplus + slot, 0, BLK_DEV - 2)
            pltpu.make_async_copy(came_ref.at[source], target, sems.at[slot]).start()

        @pl.when(slot >= surplus)
        def _():
            source = jnp.clip(slot - surplus, 0, BLK_DEV - 1)
            pltpu.make_async_copy(own_ref.at[source], target, sems.at[slot]).start()

    index, flip = swap_indices()
    rows = slots.reshape(2 * CHUNKS * 64, 128)
    for ly in range(2):
        for lz in range(8):
            slot = ly * 8 + lz
            pltpu.make_async_copy(own_ref.at[0], slots.at[ly, :, lz], sems.at[slot]).wait()

        def chunk(c, _):
            state = [swapped(rows[pl.ds((ly * CHUNKS + c) * 64 + k, 8, stride=8), :], index, flip) for k in range(FIELDS)]
            x, t = c // 2, ly * 2 + c % 2
            put(u_ref, x, t, state)
            put(w_ref, x, t, primitive(state))
            return 0

        lax.fori_loop(0, CHUNKS, chunk, 0, unroll=32)
    pack_sides(place % 2, w_ref, xl_ref, xh_ref, yn_ref, yf_ref)


def inner_kernel(w_ref, xz_ref, y_ref, half_ref, next_ref, prior_ref, flux_ref):
    row = iota(0)
    last, first = row == 7, row == 0

    def ahead(values):
        rolled = [[pltpu.roll(v, 7, 0) for v in w] for w in values]
        rolled.append(rolled[-1])
        return [[jnp.where(last, b, a) for a, b in zip(rolled[t], rolled[t + 1])] for t in range(TS)]

    def behind(values):
        rolled = [[pltpu.roll(v, 1, 0) for v in w] for w in values]
        rolled.insert(0, rolled[0])
        return [[jnp.where(first, a, b) for a, b in zip(rolled[t], rolled[t + 1])] for t in range(TS)]

    def along_y(x, _):
        prims = [cells(w_ref, x, t) for t in range(TS)]
        halves = [[0.5 * v for v in w] for w in prims]
        for t in range(TS):
            put(half_ref, x, t, halves[t])
            put(next_ref, x, t, [pltpu.roll(v, 127, 1) for v in halves[t]])
            put(prior_ref, x, t, [pltpu.roll(v, 1, 1) for v in halves[t]])
        forward = [minus(a, w) for a, w in zip(ahead(halves), halves)]
        backward = behind(forward)
        both = [edges(w, b, f) for w, b, f in zip(prims, backward, forward)]
        right = ahead([lower for _, lower in both])
        flux = [hlle(both[t][0], right[t], 1) for t in range(TS)]
        flux[0] = [jnp.where(first, 0.0, v) for v in flux[0]]
        flux[3] = [jnp.where(row >= 6, 0.0, v) for v in flux[3]]
        rolled = [[pltpu.roll(v, 1, 0) for v in w] for w in flux]
        for t in range(TS):
            if t == 0:
                before = [jnp.where(first, 0.0, v) for v in rolled[0]]
            else:
                before = [jnp.where(first, a, b) for a, b in zip(rolled[t - 1], rolled[t])]
            put(y_ref, x, t, minus(before, flux[t]))
        return 0

    lax.fori_loop(0, XS, along_y, 0, unroll=4)

    def along_z(i, _):
        x, t = i // TS, i % TS
        half = cells(half_ref, x, t)
        upper, lower = edges(cells(w_ref, x, t), minus(half, cells(prior_ref, x, t)), minus(cells(next_ref, x, t), half))
        put(flux_ref, x, t, hlle(upper, [pltpu.roll(v, 127, 1) for v in lower], 2))
        return 0

    lax.fori_loop(0, XS * TS, along_z, 0, unroll=16)

    def along_x(pair, _):
        both = (2 * pair, 2 * pair + 1)

        def store(x, t, change=None):
            total = [pltpu.roll(v, 1, 1) - v for v in cells(flux_ref, x, t)]
            put(xz_ref, x, t, total if change is None else plus(total, change))

        start = []
        for t in both:
            h0, h1, h2, h3 = [cells(half_ref, x, t) for x in range(4)]
            d1, d2 = minus(h2, h1), minus(h3, h2)
            upper, _ = edges(cells(w_ref, 1, t), minus(h1, h0), d1)
            after, lower = edges(cells(w_ref, 2, t), d1, d2)
            flux = hlle(upper, lower, 0)
            store(0, t)
            store(1, t, [-v for v in flux])
            start.append((d2, after, flux))

        def step(x, carry):
            result = []
            for t, (d, upper, flux) in zip(both, carry):
                forward = minus(cells(half_ref, x + 2, t), cells(half_ref, x + 1, t))
                after, lower = edges(cells(w_ref, x + 1, t), d, forward)
                new = hlle(upper, lower, 0)
                store(x, t, minus(flux, new))
                result.append((forward, after, new))
            return result

        for t, (_, _, flux) in zip(both, lax.fori_loop(2, 14, step, start, unroll=12)):
            store(14, t, flux)
            store(15, t)
        return 0

    lax.fori_loop(0, TS // 2, along_x, 0)


def outer_faces(six, normal):
    ds = [[0.5 * v for v in minus(six[i + 1], six[i])] for i in range(len(six) - 1)]
    both = [edges(six[i + 1], ds[i], ds[i + 1]) for i in range(len(six) - 2)]
    return [hlle(both[i][0], both[i + 1][1], normal) for i in range(len(six) - 3)]


def outer(core, w_ref, sides, xc, yc):
    xl_ref, xh_ref, yn_ref, yf_ref = sides

    def column(t, _):
        near = [cells(xl_ref, 0, t), cells(xl_ref, 1, t)] + [cells(w_ref, x, t) for x in range(3)]
        a, b = outer_faces(near, 0)
        put(xc, 0, t, minus(a, b))
        put(xc, 1, t, b)
        far = [cells(w_ref, x, t) for x in range(13, 16)] + [cells(xh_ref, 0, t), cells(xh_ref, 1, t)]
        a, b = outer_faces(far, 0)
        put(xc, 2, t, [-v for v in a])
        put(xc, 3, t, minus(a, b))
        return 0

    lax.fori_loop(0, TS, column, 0, unroll=4)
    rows = w_ref.reshape(XS * 256, 128)
    packed = yc.reshape(XS * 128, 128)
    zero = jnp.zeros((8, 128), jnp.float32)

    def clear(x, _):
        for part in range(2):
            for k in range(FIELDS):
                yc[x, part, k] = zero
        return 0

    lax.fori_loop(0, XS, clear, 0)

    def store(half, part, y, values):
        for k in range(FIELDS):
            packed[pl.ds(half * 1024 + part * 64 + k * 8 + y, 8, stride=128), :] = values[k]

    for half in range(2):
        own = lambda y: [y_layer(rows, half, k, y) for k in range(FIELDS)]
        sent = lambda layer, near: [jnp.where(near, yn_ref[layer, half, k], yf_ref[layer, half, k]) for k in range(FIELDS)]
        a, b = outer_faces([sent(0, core == 1), sent(1, core == 1), own(0), own(1), own(2)], 1)
        store(half, 0, 0, minus(a, b))
        store(half, 0, 1, b)
        a, b = outer_faces([own(29), own(30), own(31), sent(0, core == 0), sent(1, core == 0)], 1)
        store(half, 1, 6, [-v for v in a])
        store(half, 1, 7, minus(a, b))


def changes(inner, xc, yc, x, t, edge):
    xz_ref, y_ref = inner
    total = plus(cells(xz_ref, x, t), cells(y_ref, x, t))
    if t in (0, 3):
        total = plus(total, cells(yc, x, t // 3))
    if edge is not None:
        total = plus(total, cells(xc, edge, t))
    return total


def each_layer(work):
    for edge, x in enumerate((0, 1, XS - 2, XS - 1)):
        work(x, edge)
    lax.fori_loop(2, XS - 2, lambda x, _: (work(x, None), 0)[1], 0, unroll=12)


def step_of(tile_ref):
    return COURANT / jnp.max(jnp.where(iota(0) == 1, tile_ref[...], 0.0))


def first_kernel(place_ref, tile_ref, w_ref, u_ref, txz, ty, xl, xh, yn, yf, s_ref, w2_ref, xl_ref, xh_ref, yn_ref, yf_ref, xc, yc):
    step = step_of(tile_ref)
    core = place_ref[0] % 2
    outer(core, w_ref, (xl, xh, yn, yf), xc, yc)

    def work(x, edge):
        for t in range(TS):
            change = changes((txz, ty), xc, yc, x, t, edge)
            state = cells(u_ref, x, t)
            first = [u + step * c for u, c in zip(state, change)]
            put(s_ref, x, t, [0.5 * (u + f) for u, f in zip(state, first)])
            put(w2_ref, x, t, primitive(first))

    each_layer(work)
    pack_sides(core, w2_ref, xl_ref, xh_ref, yn_ref, yf_ref)


def second_kernel(place_ref, tile_ref, w_ref, s_ref, txz, ty, xl, xh, yn, yf, out_ref, xc, yc, blocks, sems):
    step = 0.5 * step_of(tile_ref)
    outer(place_ref[0] % 2, w_ref, (xl, xh, yn, yf), xc, yc)
    index, flip = swap_indices()
    rows = blocks.reshape(BLK_DEV * CHUNKS * FIELDS, 128)

    def work(x, edge):
        for t in range(TS):
            change = changes((txz, ty), xc, yc, x, t, edge)
            chunk = 2 * x + t % 2
            for k, (s, c) in enumerate(zip(cells(s_ref, x, t), change)):
                start = ((t // 2) * 8 * CHUNKS + chunk) * 8 + k
                rows[pl.ds(start, 8, stride=CHUNKS * 8), :] = swapped(s + step * c, index, flip)

    def part(quarter):
        chunks = pl.ds(quarter * 8, 8)
        return pltpu.make_async_copy(blocks.at[:, chunks], out_ref.at[:, chunks], sems.at[quarter])

    def pairs(first, last):
        lax.fori_loop(first, last, lambda x, _: (work(x, None), 0)[1], 0, unroll=last - first)

    work(0, 0)
    work(1, 1)
    pairs(2, 8)
    part(0).start()
    part(1).start()
    pairs(8, 12)
    part(2).start()
    pairs(12, 14)
    work(14, 2)
    work(15, 3)
    part(3).start()
    for quarter in range(4):
        part(quarter).wait()


VMEM = pl.BlockSpec(memory_space=pltpu.VMEM)
SMEM = pl.BlockSpec(memory_space=pltpu.SMEM)
ANY = pl.BlockSpec(memory_space=pl.ANY)
HBM = pl.BlockSpec(memory_space=pltpu.HBM)


def shape(dims):
    return pltpu.VMEM(dims, jnp.float32)


def kernel(function, in_specs, outs, scratch, name, flops, limit=LIMIT, out_spec=VMEM):
    single = not isinstance(outs, list)
    return pl.pallas_call(
        function,
        out_shape=jax.ShapeDtypeStruct(outs, jnp.float32) if out_spec is ANY else shape(outs) if single else [shape(dims) for dims in outs],
        in_specs=in_specs,
        out_specs=out_spec if single else [out_spec] * len(outs),
        scratch_shapes=scratch,
        name=name,
        compiler_params=pltpu.CompilerParams(vmem_limit_bytes=limit),
        cost_estimate=pl.CostEstimate(flops=flops, bytes_accessed=6 << 20, transcendentals=0),
    )


def shifted(value, axis, by):
    count = lax.axis_size(axis)
    return lax.ppermute(value, axis, [(i, (i + by) % count) for i in range(count)])


def exchanged(xl, xh, yn, yf):
    count = lax.axis_size("dev")
    near = [(i, i ^ 1) for i in range(count)]
    far = [(i, (i + 1) % count if i % 2 else (i - 1) % count) for i in range(count)]
    return shifted(xh, "group", 1), shifted(xl, "group", -1), lax.ppermute(yn, "dev", near), lax.ppermute(yf, "dev", far)


def body(blocks_in, counts):
    devices = lax.axis_size(AXES)
    place = lax.axis_index(AXES).astype(jnp.int32).reshape(1)
    tiles = lambda value: value.reshape(value.shape[0], FIELDS, CHUNKS, 128).swapaxes(1, 2)
    own = tiles(blocks_in)
    passed = (BLK_DEV - 1, CHUNKS, FIELDS, 128)
    there = pltpu.with_memory_space_constraint(own, pltpu.HBM)
    outgoing = kernel(outgoing_kernel, [SMEM, HBM], passed, [pltpu.SemaphoreType.DMA((BLK_DEV - 1,))], "outgoing", 1 << 10)(
        counts, there
    )
    came = lax.ppermute(outgoing, AXES, [(i, i + 1) for i in range(devices - 1)])
    tile = kernel(
        speed_kernel,
        [SMEM, SMEM, HBM],
        (8, 128),
        [
            pltpu.VMEM((blocks_in.shape[0], CHUNKS, FIELDS, 128), jnp.float32),
            pltpu.SemaphoreType.DMA((pl.cdiv(blocks_in.shape[0], 4),)),
        ],
        "signal_speed",
        1 << 20,
    )(counts, place, there)
    tile = jnp.maximum(tile, lax.ppermute(tile, AXES, [(i, i ^ 1) for i in range(devices)]))
    for masks in ROUNDS:
        tile = jnp.maximum(tile, lax.ppermute(tile, AXES, [(i, i ^ masks[i % 2]) for i in range(devices)]))
    tile = jnp.maximum(tile, lax.ppermute(tile, AXES, [(i, i ^ 1) for i in range(devices)]))
    sides = [XFACE, XFACE, YFACE, YFACE]
    u, w, *faces = kernel(
        assemble_kernel,
        [SMEM, VMEM, ANY, ANY],
        [GRID, GRID] + sides,
        [pltpu.VMEM((2, CHUNKS, 8, FIELDS, 128), jnp.float32), pltpu.SemaphoreType.DMA((BLK_DEV,))],
        "assemble",
        1 << 20,
    )(place, tile, pltpu.with_memory_space_constraint(came, pltpu.HBM), there)
    corrections = [pltpu.VMEM((4, TS, FIELDS, 8, 128), jnp.float32), pltpu.VMEM((XS, 2, FIELDS, 8, 128), jnp.float32)]
    inner = kernel(inner_kernel, [VMEM], [GRID] * 2, [pltpu.VMEM(GRID, jnp.float32)] * 4, "inner_fluxes", 40 << 20)
    specs = [SMEM] + [VMEM] * 9
    ghosts = exchanged(*faces)
    s, w2, *faces = kernel(first_kernel, specs, [GRID, GRID] + sides, corrections, "first_stage", 1 << 20)(
        place, tile, w, u, *inner(w), *ghosts
    )
    ghosts = exchanged(*faces)
    result = (BLK_DEV, CHUNKS, FIELDS, 128)
    buffers = corrections + [pltpu.VMEM(result, jnp.float32), pltpu.SemaphoreType.DMA((4,))]
    out = kernel(second_kernel, specs, result, buffers, "second_stage", 1 << 20, out_spec=ANY)(
        place, tile, w2, s, *inner(w2), *ghosts
    )
    return out.swapaxes(1, 2).reshape(BLK_DEV, FIELDS, BS * BS * BS)


def solution(mesh):
    in_specs = (P(AXES, None, None), P(AXES))
    out_specs = P(AXES, None, None)
    return jax.shard_map(body, mesh=mesh, in_specs=in_specs, out_specs=out_specs, check_vma=False)
```

```python
import functools

import jax
import jax.numpy as jnp
from jax import lax
from jax.experimental import pallas as pl
from jax.experimental.pallas import tpu as pltpu
from jax.sharding import PartitionSpec as P

BS = 16
BLK_DEV = 16
FIELDS = 8
XS = 16
TS = 4
CHUNKS = 32
AXES = ("group", "dev")
ROUNDS = ((8, 32), (24, 96), (2, 32), (6, 96), (32, 32), (96, 96))

GAMMA = 5.0 / 3.0
COURANT = 0.25
DENSITY_FLOOR = 0.05
PRESSURE_FLOOR = 0.05
TINY = 1e-37

GRID = (XS, TS, FIELDS, 8, 128)
XFACE = (2, TS, FIELDS, 8, 128)
YFACE = (2, 2, FIELDS, 8, 128)
LIMIT = 24 << 20


def iota(axis):
    return lax.broadcasted_iota(jnp.int32, (8, 128), axis)


def root(value):
    return value * lax.rsqrt(value)


def primitive(state):
    density = jnp.maximum(state[0], DENSITY_FLOOR)
    inverse = 1.0 / density
    velocity = [state[k] * inverse for k in (1, 2, 3)]
    magnetic = state[5:8]
    kinetic = 0.5 * density * (velocity[0] * velocity[0] + velocity[1] * velocity[1] + velocity[2] * velocity[2])
    field = 0.5 * (magnetic[0] * magnetic[0] + magnetic[1] * magnetic[1] + magnetic[2] * magnetic[2])
    pressure = jnp.maximum((GAMMA - 1.0) * (state[4] - kinetic - field), PRESSURE_FLOOR)
    return [density] + velocity + [pressure] + list(magnetic)


def fast_speed(prims, normal, inverse, half):
    magnetic = prims[5:8]
    along = magnetic[normal] * magnetic[normal] * inverse
    sound = (0.5 * GAMMA * prims[4]) * inverse
    total = sound + half * inverse
    inner = jnp.maximum(total * total - (2.0 * sound) * along, TINY)
    return root(total + root(inner))


def half_square(field):
    return 0.5 * (field[0] * field[0] + field[1] * field[1] + field[2] * field[2])


def side(prims, normal):
    density, pressure = prims[0], prims[4]
    velocity, magnetic = prims[1:4], prims[5:8]
    half = half_square(magnetic)
    fast = fast_speed(prims, normal, 1.0 / density, half)
    total = pressure + half
    motion = velocity[0] * velocity[0] + velocity[1] * velocity[1] + velocity[2] * velocity[2]
    energy = total + 0.5 * (pressure + density * motion)
    cross = velocity[0] * magnetic[0] + velocity[1] * magnetic[1] + velocity[2] * magnetic[2]
    return fast, total, energy, cross


def weighed(prims, normal, weight, other, total, energy, cross):
    density = prims[0]
    velocity, magnetic = prims[1:4], prims[5:8]
    carried = weight * (velocity[normal] - other)
    bent = weight * magnetic[normal]
    mass = carried * density
    push = weight * total
    momentum = [mass * velocity[k] - bent * magnetic[k] for k in range(3)]
    momentum[normal] = momentum[normal] + push
    power = carried * energy + push * velocity[normal] - bent * cross
    induced = [carried * magnetic[k] - bent * velocity[k] for k in range(3)]
    induced[normal] = other * bent
    return [mass] + momentum + [power] + induced


def hlle(left, right, normal):
    fast_l, total_l, energy_l, cross_l = side(left, normal)
    fast_r, total_r, energy_r, cross_r = side(right, normal)
    speed_l, speed_r = left[1 + normal], right[1 + normal]
    upper = jnp.maximum(jnp.maximum(speed_r + fast_r, speed_l + fast_l), 0.0)
    lower = jnp.minimum(jnp.minimum(speed_l - fast_l, speed_r - fast_r), 0.0)
    weight = upper * (1.0 / (upper - lower))
    part_l = weighed(left, normal, weight, lower, total_l, energy_l, cross_l)
    part_r = weighed(right, normal, 1.0 - weight, upper, total_r, energy_r, cross_r)
    flux = [a + b for a, b in zip(part_l, part_r)]
    flux[5 + normal] = -flux[5 + normal]
    return flux


def minus(first, second):
    return [a - b for a, b in zip(first, second)]


def plus(first, second):
    return [a + b for a, b in zip(first, second)]


def edges(prims, backward, forward):
    upper, lower = [], []
    for w, a, b in zip(prims, backward, forward):
        half = jnp.maximum(jnp.minimum(a, b), jnp.minimum(jnp.maximum(a, b), 0.0))
        upper.append(w + half)
        lower.append(w - half)
    return upper, lower


def cells(ref, x, t):
    return [ref[x, t, k] for k in range(FIELDS)]


def put(ref, x, t, values):
    for k in range(FIELDS):
        ref[x, t, k] = values[k]


def outgoing_kernel(count_ref, blocks_ref, out_ref, sems):
    count, places = count_ref[0], BLK_DEV - 1

    def each(work):
        for place in range(places):
            slot = count - places + place

            @pl.when(slot >= 0)
            def _():
                source = jnp.clip(slot, 0, blocks_ref.shape[0] - 1)
                work(pltpu.make_async_copy(blocks_ref.at[source], out_ref.at[place], sems.at[place]))

    each(lambda copy: copy.start())
    each(lambda copy: copy.wait())


def speed_kernel(count_ref, place_ref, blocks_ref, tile_ref, slots, sems):
    count = count_ref[0]
    group = 4
    groups = pl.cdiv(blocks_ref.shape[0], group)

    def incoming(index, work):
        size = min(group, blocks_ref.shape[0] - index * group)
        part = pl.ds(index * group, size)

        @pl.when(index * group < count)
        def _():
            work(pltpu.make_async_copy(blocks_ref.at[part], slots.at[part], sems.at[index]))

    for index in range(groups):
        incoming(index, lambda copy: copy.start())

    rows = slots.reshape(slots.shape[0] * CHUNKS * FIELDS, 128)

    def speeds(start, tops):
        prims = primitive([rows[pl.ds(start + k, 8, stride=8), :] for k in range(FIELDS)])
        half = half_square(prims[5:8])
        inverse = 1.0 / prims[0]
        for normal in range(3):
            speed = jnp.abs(prims[1 + normal]) + fast_speed(prims, normal, inverse, half)
            tops[normal] = jnp.maximum(tops[normal], speed)

    def several(index, tops):
        for which in range(groups):
            @pl.when(index == which)
            def _():
                incoming(which, lambda copy: copy.wait())
        tops = list(tops)
        for which in range(group):
            slot = jnp.minimum(index * group + which, count - 1)
            for part in range(4):
                speeds(slot * (CHUNKS * FIELDS) + part * 64, tops)
        return tuple(tops)

    tops = lax.fori_loop(0, pl.cdiv(count, group), several, (jnp.zeros((8, 128), jnp.float32),) * 3)
    fastest = jnp.max(jnp.maximum(jnp.maximum(tops[0], tops[1]), tops[2]))
    counted = jnp.where(iota(1) == place_ref[0], count.astype(jnp.float32), 0.0)
    tile_ref[...] = jnp.where(iota(0) == 0, counted, fastest)


def swapped(value, index, flip):
    value = pltpu.roll(value, 0, 1, stride=16, stride_axis=0)
    value = jnp.take_along_axis(value, index, axis=0, mode="promise_in_bounds")
    value = pltpu.roll(value, 16, 1, stride=16, stride_axis=0)
    return jnp.take_along_axis(value, flip, axis=0, mode="promise_in_bounds")


def swap_indices():
    row, group = iota(0), iota(1) // 16
    flip = 7 - row
    return (group - flip) & 7, flip


def pack_sides(core, w_ref, xl_ref, xh_ref, yn_ref, yf_ref):
    for layer in range(2):
        for t in range(TS):
            put(xl_ref, layer, t, cells(w_ref, layer, t))
            put(xh_ref, layer, t, cells(w_ref, XS - 2 + layer, t))
    rows = w_ref.reshape(XS * 256, 128)
    high = y_offset(30)
    for layer in range(2):
        for half in range(2):
            for k in range(FIELDS):
                start = half * 2048 + k * 8 + layer
                yn_ref[layer, half, k] = rows[pl.ds(start + (1 - core) * high, 8, stride=256), :]
                yf_ref[layer, half, k] = rows[pl.ds(start + core * high, 8, stride=256), :]


def y_offset(y):
    return (y // 8) * 64 + y % 8


def y_layer(rows, half, k, y):
    return rows[pl.ds(half * 2048 + k * 8 + y_offset(y), 8, stride=256), :]


def assemble_kernel(place_ref, tile_ref, came_ref, own_ref, u_ref, w_ref, xl_ref, xh_ref, yn_ref, yf_ref, slots, sems):
    place = place_ref[0]
    earlier = jnp.where((iota(0) == 0) & (iota(1) < place), tile_ref[...], 0.0)
    surplus = jnp.sum(earlier).astype(jnp.int32) - place * BLK_DEV

    for slot in range(BLK_DEV):
        target = slots.at[slot // 8, :, slot % 8]

        @pl.when(slot < surplus)
        def _():
            source = jnp.clip(BLK_DEV - 1 - surplus + slot, 0, BLK_DEV - 2)
            pltpu.make_async_copy(came_ref.at[source], target, sems.at[slot]).start()

        @pl.when(slot >= surplus)
        def _():
            source = jnp.clip(slot - surplus, 0, BLK_DEV - 1)
            pltpu.make_async_copy(own_ref.at[source], target, sems.at[slot]).start()

    index, flip = swap_indices()
    rows = slots.reshape(2 * CHUNKS * 64, 128)
    for ly in range(2):
        for lz in range(8):
            slot = ly * 8 + lz
            pltpu.make_async_copy(own_ref.at[0], slots.at[ly, :, lz], sems.at[slot]).wait()

        def chunk(c, _):
            state = [swapped(rows[pl.ds((ly * CHUNKS + c) * 64 + k, 8, stride=8), :], index, flip) for k in range(FIELDS)]
            x, t = c // 2, ly * 2 + c % 2
            put(u_ref, x, t, state)
            put(w_ref, x, t, primitive(state))
            return 0

        lax.fori_loop(0, CHUNKS, chunk, 0, unroll=32)
    pack_sides(place % 2, w_ref, xl_ref, xh_ref, yn_ref, yf_ref)


def inner_kernel(w_ref, xz_ref, y_ref, half_ref, next_ref, prior_ref, flux_ref):
    row = iota(0)
    last, first = row == 7, row == 0

    def ahead(values):
        rolled = [[pltpu.roll(v, 7, 0) for v in w] for w in values]
        rolled.append(rolled[-1])
        return [[jnp.where(last, b, a) for a, b in zip(rolled[t], rolled[t + 1])] for t in range(TS)]

    def behind(values):
        rolled = [[pltpu.roll(v, 1, 0) for v in w] for w in values]
        rolled.insert(0, rolled[0])
        return [[jnp.where(first, a, b) for a, b in zip(rolled[t], rolled[t + 1])] for t in range(TS)]

    def along_y(x, _):
        prims = [cells(w_ref, x, t) for t in range(TS)]
        halves = [[0.5 * v for v in w] for w in prims]
        for t in range(TS):
            put(half_ref, x, t, halves[t])
            put(next_ref, x, t, [pltpu.roll(v, 127, 1) for v in halves[t]])
            put(prior_ref, x, t, [pltpu.roll(v, 1, 1) for v in halves[t]])
        forward = [minus(a, w) for a, w in zip(ahead(halves), halves)]
        backward = behind(forward)
        both = [edges(w, b, f) for w, b, f in zip(prims, backward, forward)]
        right = ahead([lower for _, lower in both])
        flux = [hlle(both[t][0], right[t], 1) for t in range(TS)]
        flux[0] = [jnp.where(first, 0.0, v) for v in flux[0]]
        flux[3] = [jnp.where(row >= 6, 0.0, v) for v in flux[3]]
        rolled = [[pltpu.roll(v, 1, 0) for v in w] for w in flux]
        for t in range(TS):
            if t == 0:
                before = [jnp.where(first, 0.0, v) for v in rolled[0]]
            else:
                before = [jnp.where(first, a, b) for a, b in zip(rolled[t - 1], rolled[t])]
            put(y_ref, x, t, minus(before, flux[t]))
        return 0

    lax.fori_loop(0, XS, along_y, 0, unroll=4)

    def along_z(i, _):
        x, t = i // TS, i % TS
        half = cells(half_ref, x, t)
        upper, lower = edges(cells(w_ref, x, t), minus(half, cells(prior_ref, x, t)), minus(cells(next_ref, x, t), half))
        put(flux_ref, x, t, hlle(upper, [pltpu.roll(v, 127, 1) for v in lower], 2))
        return 0

    lax.fori_loop(0, XS * TS, along_z, 0, unroll=16)

    def along_x(pair, _):
        both = (2 * pair, 2 * pair + 1)

        def store(x, t, change=None):
            total = [pltpu.roll(v, 1, 1) - v for v in cells(flux_ref, x, t)]
            put(xz_ref, x, t, total if change is None else plus(total, change))

        start = []
        for t in both:
            h0, h1, h2, h3 = [cells(half_ref, x, t) for x in range(4)]
            d1, d2 = minus(h2, h1), minus(h3, h2)
            upper, _ = edges(cells(w_ref, 1, t), minus(h1, h0), d1)
            after, lower = edges(cells(w_ref, 2, t), d1, d2)
            flux = hlle(upper, lower, 0)
            store(0, t)
            store(1, t, [-v for v in flux])
            start.append((d2, after, flux))

        def step(x, carry):
            result = []
            for t, (d, upper, flux) in zip(both, carry):
                forward = minus(cells(half_ref, x + 2, t), cells(half_ref, x + 1, t))
                after, lower = edges(cells(w_ref, x + 1, t), d, forward)
                new = hlle(upper, lower, 0)
                store(x, t, minus(flux, new))
                result.append((forward, after, new))
            return result

        for t, (_, _, flux) in zip(both, lax.fori_loop(2, 14, step, start, unroll=12)):
            store(14, t, flux)
            store(15, t)
        return 0

    lax.fori_loop(0, TS // 2, along_x, 0)


def outer_faces(six, normal):
    ds = [[0.5 * v for v in minus(six[i + 1], six[i])] for i in range(len(six) - 1)]
    both = [edges(six[i + 1], ds[i], ds[i + 1]) for i in range(len(six) - 2)]
    return [hlle(both[i][0], both[i + 1][1], normal) for i in range(len(six) - 3)]


def outer(core, w_ref, sides, xc, yc):
    xl_ref, xh_ref, yn_ref, yf_ref = sides

    def column(t, _):
        near = [cells(xl_ref, 0, t), cells(xl_ref, 1, t)] + [cells(w_ref, x, t) for x in range(3)]
        a, b = outer_faces(near, 0)
        put(xc, 0, t, minus(a, b))
        put(xc, 1, t, b)
        far = [cells(w_ref, x, t) for x in range(13, 16)] + [cells(xh_ref, 0, t), cells(xh_ref, 1, t)]
        a, b = outer_faces(far, 0)
        put(xc, 2, t, [-v for v in a])
        put(xc, 3, t, minus(a, b))
        return 0

    lax.fori_loop(0, TS, column, 0, unroll=4)
    rows = w_ref.reshape(XS * 256, 128)
    packed = yc.reshape(XS * 128, 128)
    zero = jnp.zeros((8, 128), jnp.float32)

    def clear(x, _):
        for part in range(2):
            for k in range(FIELDS):
                yc[x, part, k] = zero
        return 0

    lax.fori_loop(0, XS, clear, 0)

    def store(half, part, y, values):
        for k in range(FIELDS):
            packed[pl.ds(half * 1024 + part * 64 + k * 8 + y, 8, stride=128), :] = values[k]

    for half in range(2):
        own = lambda y: [y_layer(rows, half, k, y) for k in range(FIELDS)]
        sent = lambda layer, near: [jnp.where(near, yn_ref[layer, half, k], yf_ref[layer, half, k]) for k in range(FIELDS)]
        a, b = outer_faces([sent(0, core == 1), sent(1, core == 1), own(0), own(1), own(2)], 1)
        store(half, 0, 0, minus(a, b))
        store(half, 0, 1, b)
        a, b = outer_faces([own(29), own(30), own(31), sent(0, core == 0), sent(1, core == 0)], 1)
        store(half, 1, 6, [-v for v in a])
        store(half, 1, 7, minus(a, b))


def changes(inner, xc, yc, x, t, edge):
    xz_ref, y_ref = inner
    total = plus(cells(xz_ref, x, t), cells(y_ref, x, t))
    if t in (0, 3):
        total = plus(total, cells(yc, x, t // 3))
    if edge is not None:
        total = plus(total, cells(xc, edge, t))
    return total


def each_layer(work):
    for edge, x in enumerate((0, 1, XS - 2, XS - 1)):
        work(x, edge)
    lax.fori_loop(2, XS - 2, lambda x, _: (work(x, None), 0)[1], 0, unroll=12)


def step_of(tile_ref):
    return COURANT / jnp.max(jnp.where(iota(0) == 1, tile_ref[...], 0.0))


def first_kernel(place_ref, tile_ref, w_ref, u_ref, txz, ty, xl, xh, yn, yf, s_ref, w2_ref, xl_ref, xh_ref, yn_ref, yf_ref, xc, yc):
    step = step_of(tile_ref)
    core = place_ref[0] % 2
    outer(core, w_ref, (xl, xh, yn, yf), xc, yc)

    def work(x, edge):
        for t in range(TS):
            change = changes((txz, ty), xc, yc, x, t, edge)
            state = cells(u_ref, x, t)
            first = [u + step * c for u, c in zip(state, change)]
            put(s_ref, x, t, [0.5 * (u + f) for u, f in zip(state, first)])
            put(w2_ref, x, t, primitive(first))

    each_layer(work)
    pack_sides(core, w2_ref, xl_ref, xh_ref, yn_ref, yf_ref)


def second_kernel(place_ref, tile_ref, w_ref, s_ref, txz, ty, xl, xh, yn, yf, out_ref, xc, yc, blocks, sems):
    step = 0.5 * step_of(tile_ref)
    outer(place_ref[0] % 2, w_ref, (xl, xh, yn, yf), xc, yc)
    index, flip = swap_indices()
    rows = blocks.reshape(BLK_DEV * CHUNKS * FIELDS, 128)

    def work(x, edge):
        for t in range(TS):
            change = changes((txz, ty), xc, yc, x, t, edge)
            chunk = 2 * x + t % 2
            for k, (s, c) in enumerate(zip(cells(s_ref, x, t), change)):
                start = ((t // 2) * 8 * CHUNKS + chunk) * 8 + k
                rows[pl.ds(start, 8, stride=CHUNKS * 8), :] = swapped(s + step * c, index, flip)

    def part(quarter):
        chunks = pl.ds(quarter * 8, 8)
        return pltpu.make_async_copy(blocks.at[:, chunks], out_ref.at[:, chunks], sems.at[quarter])

    def pairs(first, last):
        lax.fori_loop(first, last, lambda x, _: (work(x, None), 0)[1], 0, unroll=last - first)

    work(0, 0)
    work(1, 1)
    pairs(2, 8)
    part(0).start()
    part(1).start()
    pairs(8, 12)
    part(2).start()
    pairs(12, 14)
    work(14, 2)
    work(15, 3)
    part(3).start()
    for quarter in range(4):
        part(quarter).wait()


VMEM = pl.BlockSpec(memory_space=pltpu.VMEM)
SMEM = pl.BlockSpec(memory_space=pltpu.SMEM)
ANY = pl.BlockSpec(memory_space=pl.ANY)
HBM = pl.BlockSpec(memory_space=pltpu.HBM)


def shape(dims):
    return pltpu.VMEM(dims, jnp.float32)


def kernel(function, in_specs, outs, scratch, name, flops, limit=LIMIT, out_spec=VMEM):
    single = not isinstance(outs, list)
    return pl.pallas_call(
        function,
        out_shape=jax.ShapeDtypeStruct(outs, jnp.float32) if out_spec is ANY else shape(outs) if single else [shape(dims) for dims in outs],
        in_specs=in_specs,
        out_specs=out_spec if single else [out_spec] * len(outs),
        scratch_shapes=scratch,
        name=name,
        compiler_params=pltpu.CompilerParams(vmem_limit_bytes=limit),
        cost_estimate=pl.CostEstimate(flops=flops, bytes_accessed=6 << 20, transcendentals=0),
    )


def shifted(value, axis, by):
    count = lax.axis_size(axis)
    return lax.ppermute(value, axis, [(i, (i + by) % count) for i in range(count)])


def exchanged(xl, xh, yn, yf):
    count = lax.axis_size("dev")
    near = [(i, i ^ 1) for i in range(count)]
    far = [(i, (i + 1) % count if i % 2 else (i - 1) % count) for i in range(count)]
    return shifted(xh, "group", 1), shifted(xl, "group", -1), lax.ppermute(yn, "dev", near), lax.ppermute(yf, "dev", far)


def body(blocks_in, counts):
    devices = lax.axis_size(AXES)
    place = lax.axis_index(AXES).astype(jnp.int32).reshape(1)
    tiles = lambda value: value.reshape(value.shape[0], FIELDS, CHUNKS, 128).swapaxes(1, 2)
    own = tiles(blocks_in)
    passed = (BLK_DEV - 1, CHUNKS, FIELDS, 128)
    there = pltpu.with_memory_space_constraint(own, pltpu.HBM)
    outgoing = kernel(outgoing_kernel, [SMEM, HBM], passed, [pltpu.SemaphoreType.DMA((BLK_DEV - 1,))], "outgoing", 1 << 10)(
        counts, there
    )
    came = lax.ppermute(outgoing, AXES, [(i, i + 1) for i in range(devices - 1)])
    tile = kernel(
        speed_kernel,
        [SMEM, SMEM, HBM],
        (8, 128),
        [
            pltpu.VMEM((blocks_in.shape[0], CHUNKS, FIELDS, 128), jnp.float32),
            pltpu.SemaphoreType.DMA((pl.cdiv(blocks_in.shape[0], 4),)),
        ],
        "signal_speed",
        1 << 20,
    )(counts, place, there)
    tile = jnp.maximum(tile, lax.ppermute(tile, AXES, [(i, i ^ 1) for i in range(devices)]))
    for masks in ROUNDS:
        tile = jnp.maximum(tile, lax.ppermute(tile, AXES, [(i, i ^ masks[i % 2]) for i in range(devices)]))
    tile = jnp.maximum(tile, lax.ppermute(tile, AXES, [(i, i ^ 1) for i in range(devices)]))
    sides = [XFACE, XFACE, YFACE, YFACE]
    u, w, *faces = kernel(
        assemble_kernel,
        [SMEM, VMEM, ANY, ANY],
        [GRID, GRID] + sides,
        [pltpu.VMEM((2, CHUNKS, 8, FIELDS, 128), jnp.float32), pltpu.SemaphoreType.DMA((BLK_DEV,))],
        "assemble",
        1 << 20,
    )(place, tile, pltpu.with_memory_space_constraint(came, pltpu.HBM), there)
    corrections = [pltpu.VMEM((4, TS, FIELDS, 8, 128), jnp.float32), pltpu.VMEM((XS, 2, FIELDS, 8, 128), jnp.float32)]
    inner = kernel(inner_kernel, [VMEM], [GRID] * 2, [pltpu.VMEM(GRID, jnp.float32)] * 4, "inner_fluxes", 40 << 20)
    specs = [SMEM] + [VMEM] * 9
    ghosts = exchanged(*faces)
    s, w2, *faces = kernel(first_kernel, specs, [GRID, GRID] + sides, corrections, "first_stage", 1 << 20)(
        place, tile, w, u, *inner(w), *ghosts
    )
    ghosts = exchanged(*faces)
    result = (BLK_DEV, CHUNKS, FIELDS, 128)
    buffers = corrections + [pltpu.VMEM(result, jnp.float32), pltpu.SemaphoreType.DMA((4,))]
    out = kernel(second_kernel, specs, result, buffers, "second_stage", 1 << 20, out_spec=ANY)(
        place, tile, w2, s, *inner(w2), *ghosts
    )
    return out.swapaxes(1, 2).reshape(BLK_DEV, FIELDS, BS * BS * BS)


def solution(mesh):
    in_specs = (P(AXES, None, None), P(AXES))
    out_specs = P(AXES, None, None)
    return jax.shard_map(body, mesh=mesh, in_specs=in_specs, out_specs=out_specs, check_vma=False)
```

```python
import functools

import jax
import jax.numpy as jnp
from jax import lax
from jax.experimental import pallas as pl
from jax.experimental.pallas import tpu as pltpu
from jax.sharding import PartitionSpec as P

BS = 16
BLK_DEV = 16
FIELDS = 8
XS = 16
TS = 4
CHUNKS = 32
AXES = ("group", "dev")
ROUNDS = ((8, 32), (24, 96), (2, 32), (6, 96), (32, 32), (96, 96))

GAMMA = 5.0 / 3.0
COURANT = 0.25
DENSITY_FLOOR = 0.05
PRESSURE_FLOOR = 0.05
TINY = 1e-37

GRID = (XS, TS, FIELDS, 8, 128)
XFACE = (2, TS, FIELDS, 8, 128)
YFACE = (2, 2, FIELDS, 8, 128)
LIMIT = 24 << 20


def iota(axis):
    return lax.broadcasted_iota(jnp.int32, (8, 128), axis)


def root(value):
    return value * lax.rsqrt(value)


def primitive(state):
    density = jnp.maximum(state[0], DENSITY_FLOOR)
    inverse = 1.0 / density
    velocity = [state[k] * inverse for k in (1, 2, 3)]
    magnetic = state[5:8]
    kinetic = 0.5 * density * (velocity[0] * velocity[0] + velocity[1] * velocity[1] + velocity[2] * velocity[2])
    field = 0.5 * (magnetic[0] * magnetic[0] + magnetic[1] * magnetic[1] + magnetic[2] * magnetic[2])
    pressure = jnp.maximum((GAMMA - 1.0) * (state[4] - kinetic - field), PRESSURE_FLOOR)
    return [density] + velocity + [pressure] + list(magnetic)


def fast_speed(prims, normal, inverse, half):
    magnetic = prims[5:8]
    along = magnetic[normal] * magnetic[normal] * inverse
    sound = (0.5 * GAMMA * prims[4]) * inverse
    total = sound + half * inverse
    inner = jnp.maximum(total * total - (2.0 * sound) * along, TINY)
    return root(total + root(inner))


def half_square(field):
    return 0.5 * (field[0] * field[0] + field[1] * field[1] + field[2] * field[2])


def side(prims, normal):
    density, pressure = prims[0], prims[4]
    velocity, magnetic = prims[1:4], prims[5:8]
    half = half_square(magnetic)
    fast = fast_speed(prims, normal, 1.0 / density, half)
    total = pressure + half
    motion = velocity[0] * velocity[0] + velocity[1] * velocity[1] + velocity[2] * velocity[2]
    energy = total + 0.5 * (pressure + density * motion)
    cross = velocity[0] * magnetic[0] + velocity[1] * magnetic[1] + velocity[2] * magnetic[2]
    return fast, total, energy, cross


def weighed(prims, normal, weight, other, total, energy, cross):
    density = prims[0]
    velocity, magnetic = prims[1:4], prims[5:8]
    carried = weight * (velocity[normal] - other)
    bent = weight * magnetic[normal]
    mass = carried * density
    push = weight * total
    momentum = [mass * velocity[k] - bent * magnetic[k] for k in range(3)]
    momentum[normal] = momentum[normal] + push
    power = carried * energy + push * velocity[normal] - bent * cross
    induced = [carried * magnetic[k] - bent * velocity[k] for k in range(3)]
    induced[normal] = other * bent
    return [mass] + momentum + [power] + induced


def hlle(left, right, normal):
    fast_l, total_l, energy_l, cross_l = side(left, normal)
    fast_r, total_r, energy_r, cross_r = side(right, normal)
    speed_l, speed_r = left[1 + normal], right[1 + normal]
    upper = jnp.maximum(jnp.maximum(speed_r + fast_r, speed_l + fast_l), 0.0)
    lower = jnp.minimum(jnp.minimum(speed_l - fast_l, speed_r - fast_r), 0.0)
    weight = upper * (1.0 / (upper - lower))
    part_l = weighed(left, normal, weight, lower, total_l, energy_l, cross_l)
    part_r = weighed(right, normal, 1.0 - weight, upper, total_r, energy_r, cross_r)
    flux = [a + b for a, b in zip(part_l, part_r)]
    flux[5 + normal] = -flux[5 + normal]
    return flux


def minus(first, second):
    return [a - b for a, b in zip(first, second)]


def plus(first, second):
    return [a + b for a, b in zip(first, second)]


def edges(prims, backward, forward):
    upper, lower = [], []
    for w, a, b in zip(prims, backward, forward):
        half = jnp.maximum(jnp.minimum(a, b), jnp.minimum(jnp.maximum(a, b), 0.0))
        upper.append(w + half)
        lower.append(w - half)
    return upper, lower


def cells(ref, x, t):
    return [ref[x, t, k] for k in range(FIELDS)]


def put(ref, x, t, values):
    for k in range(FIELDS):
        ref[x, t, k] = values[k]


def outgoing_kernel(count_ref, blocks_ref, out_ref, sems):
    count, places = count_ref[0], BLK_DEV - 1

    def each(work):
        for place in range(places):
            slot = count - places + place

            @pl.when(slot >= 0)
            def _():
                source = jnp.clip(slot, 0, blocks_ref.shape[0] - 1)
                work(pltpu.make_async_copy(blocks_ref.at[source], out_ref.at[place], sems.at[place]))

    each(lambda copy: copy.start())
    each(lambda copy: copy.wait())


def speed_kernel(count_ref, place_ref, blocks_ref, tile_ref, slots, sems):
    count = count_ref[0]
    group = 4
    groups = pl.cdiv(blocks_ref.shape[0], group)

    def incoming(index, work):
        size = min(group, blocks_ref.shape[0] - index * group)
        part = pl.ds(index * group, size)

        @pl.when(index * group < count)
        def _():
            work(pltpu.make_async_copy(blocks_ref.at[part], slots.at[part], sems.at[index]))

    for index in range(groups):
        incoming(index, lambda copy: copy.start())

    rows = slots.reshape(slots.shape[0] * CHUNKS * FIELDS, 128)

    def speeds(start, tops):
        prims = primitive([rows[pl.ds(start + k, 8, stride=8), :] for k in range(FIELDS)])
        half = half_square(prims[5:8])
        inverse = 1.0 / prims[0]
        for normal in range(3):
            speed = jnp.abs(prims[1 + normal]) + fast_speed(prims, normal, inverse, half)
            tops[normal] = jnp.maximum(tops[normal], speed)

    def several(index, tops):
        for which in range(groups):
            @pl.when(index == which)
            def _():
                incoming(which, lambda copy: copy.wait())
        tops = list(tops)
        for which in range(group):
            slot = jnp.minimum(index * group + which, count - 1)
            for part in range(4):
                speeds(slot * (CHUNKS * FIELDS) + part * 64, tops)
        return tuple(tops)

    tops = lax.fori_loop(0, pl.cdiv(count, group), several, (jnp.zeros((8, 128), jnp.float32),) * 3)
    fastest = jnp.max(jnp.maximum(jnp.maximum(tops[0], tops[1]), tops[2]))
    counted = jnp.where(iota(1) == place_ref[0], count.astype(jnp.float32), 0.0)
    tile_ref[...] = jnp.where(iota(0) == 0, counted, fastest)


def swapped(value, index, flip):
    value = pltpu.roll(value, 0, 1, stride=16, stride_axis=0)
    value = jnp.take_along_axis(value, index, axis=0, mode="promise_in_bounds")
    value = pltpu.roll(value, 16, 1, stride=16, stride_axis=0)
    return jnp.take_along_axis(value, flip, axis=0, mode="promise_in_bounds")


def swap_indices():
    row, group = iota(0), iota(1) // 16
    flip = 7 - row
    return (group - flip) & 7, flip


def pack_sides(core, w_ref, xl_ref, xh_ref, yn_ref, yf_ref):
    for layer in range(2):
        for t in range(TS):
            put(xl_ref, layer, t, cells(w_ref, layer, t))
            put(xh_ref, layer, t, cells(w_ref, XS - 2 + layer, t))
    rows = w_ref.reshape(XS * 256, 128)
    high = y_offset(30)
    for layer in range(2):
        for half in range(2):
            for k in range(FIELDS):
                start = half * 2048 + k * 8 + layer
                yn_ref[layer, half, k] = rows[pl.ds(start + (1 - core) * high, 8, stride=256), :]
                yf_ref[layer, half, k] = rows[pl.ds(start + core * high, 8, stride=256), :]


def y_offset(y):
    return (y // 8) * 64 + y % 8


def y_layer(rows, half, k, y):
    return rows[pl.ds(half * 2048 + k * 8 + y_offset(y), 8, stride=256), :]


def assemble_kernel(place_ref, tile_ref, came_ref, own_ref, u_ref, w_ref, xl_ref, xh_ref, yn_ref, yf_ref, slots, sems):
    place = place_ref[0]
    earlier = jnp.where((iota(0) == 0) & (iota(1) < place), tile_ref[...], 0.0)
    surplus = jnp.sum(earlier).astype(jnp.int32) - place * BLK_DEV

    for slot in range(BLK_DEV):
        target = slots.at[slot // 8, :, slot % 8]

        @pl.when(slot < surplus)
        def _():
            source = jnp.clip(BLK_DEV - 1 - surplus + slot, 0, BLK_DEV - 2)
            pltpu.make_async_copy(came_ref.at[source], target, sems.at[slot]).start()

        @pl.when(slot >= surplus)
        def _():
            source = jnp.clip(slot - surplus, 0, BLK_DEV - 1)
            pltpu.make_async_copy(own_ref.at[source], target, sems.at[slot]).start()

    index, flip = swap_indices()
    rows = slots.reshape(2 * CHUNKS * 64, 128)
    for ly in range(2):
        for lz in range(8):
            slot = ly * 8 + lz
            pltpu.make_async_copy(own_ref.at[0], slots.at[ly, :, lz], sems.at[slot]).wait()

        def chunk(c, _):
            state = [swapped(rows[pl.ds((ly * CHUNKS + c) * 64 + k, 8, stride=8), :], index, flip) for k in range(FIELDS)]
            x, t = c // 2, ly * 2 + c % 2
            put(u_ref, x, t, state)
            put(w_ref, x, t, primitive(state))
            return 0

        lax.fori_loop(0, CHUNKS, chunk, 0, unroll=32)
    pack_sides(place % 2, w_ref, xl_ref, xh_ref, yn_ref, yf_ref)


def inner_kernel(w_ref, xz_ref, y_ref, half_ref, next_ref, prior_ref, flux_ref):
    row = iota(0)
    last, first = row == 7, row == 0

    def ahead(values):
        rolled = [[pltpu.roll(v, 7, 0) for v in w] for w in values]
        rolled.append(rolled[-1])
        return [[jnp.where(last, b, a) for a, b in zip(rolled[t], rolled[t + 1])] for t in range(TS)]

    def behind(values):
        rolled = [[pltpu.roll(v, 1, 0) for v in w] for w in values]
        rolled.insert(0, rolled[0])
        return [[jnp.where(first, a, b) for a, b in zip(rolled[t], rolled[t + 1])] for t in range(TS)]

    def along_y(x, _):
        prims = [cells(w_ref, x, t) for t in range(TS)]
        halves = [[0.5 * v for v in w] for w in prims]
        for t in range(TS):
            put(half_ref, x, t, halves[t])
            put(next_ref, x, t, [pltpu.roll(v, 127, 1) for v in halves[t]])
            put(prior_ref, x, t, [pltpu.roll(v, 1, 1) for v in halves[t]])
        forward = [minus(a, w) for a, w in zip(ahead(halves), halves)]
        backward = behind(forward)
        both = [edges(w, b, f) for w, b, f in zip(prims, backward, forward)]
        right = ahead([lower for _, lower in both])
        flux = [hlle(both[t][0], right[t], 1) for t in range(TS)]
        flux[0] = [jnp.where(first, 0.0, v) for v in flux[0]]
        flux[3] = [jnp.where(row >= 6, 0.0, v) for v in flux[3]]
        rolled = [[pltpu.roll(v, 1, 0) for v in w] for w in flux]
        for t in range(TS):
            if t == 0:
                before = [jnp.where(first, 0.0, v) for v in rolled[0]]
            else:
                before = [jnp.where(first, a, b) for a, b in zip(rolled[t - 1], rolled[t])]
            put(y_ref, x, t, minus(before, flux[t]))
        return 0

    lax.fori_loop(0, XS, along_y, 0, unroll=4)

    def along_z(i, _):
        x, t = i // TS, i % TS
        half = cells(half_ref, x, t)
        upper, lower = edges(cells(w_ref, x, t), minus(half, cells(prior_ref, x, t)), minus(cells(next_ref, x, t), half))
        put(flux_ref, x, t, hlle(upper, [pltpu.roll(v, 127, 1) for v in lower], 2))
        return 0

    lax.fori_loop(0, XS * TS, along_z, 0, unroll=16)

    def along_x(pair, _):
        both = (2 * pair, 2 * pair + 1)

        def store(x, t, change=None):
            total = [pltpu.roll(v, 1, 1) - v for v in cells(flux_ref, x, t)]
            put(xz_ref, x, t, total if change is None else plus(total, change))

        start = []
        for t in both:
            h0, h1, h2, h3 = [cells(half_ref, x, t) for x in range(4)]
            d1, d2 = minus(h2, h1), minus(h3, h2)
            upper, _ = edges(cells(w_ref, 1, t), minus(h1, h0), d1)
            after, lower = edges(cells(w_ref, 2, t), d1, d2)
            flux = hlle(upper, lower, 0)
            store(0, t)
            store(1, t, [-v for v in flux])
            start.append((d2, after, flux))

        def step(x, carry):
            result = []
            for t, (d, upper, flux) in zip(both, carry):
                forward = minus(cells(half_ref, x + 2, t), cells(half_ref, x + 1, t))
                after, lower = edges(cells(w_ref, x + 1, t), d, forward)
                new = hlle(upper, lower, 0)
                store(x, t, minus(flux, new))
                result.append((forward, after, new))
            return result

        for t, (_, _, flux) in zip(both, lax.fori_loop(2, 14, step, start, unroll=12)):
            store(14, t, flux)
            store(15, t)
        return 0

    lax.fori_loop(0, TS // 2, along_x, 0)


def outer_faces(six, normal):
    ds = [[0.5 * v for v in minus(six[i + 1], six[i])] for i in range(len(six) - 1)]
    both = [edges(six[i + 1], ds[i], ds[i + 1]) for i in range(len(six) - 2)]
    return [hlle(both[i][0], both[i + 1][1], normal) for i in range(len(six) - 3)]


def outer(core, w_ref, sides, xc, yc):
    xl_ref, xh_ref, yn_ref, yf_ref = sides

    def column(t, _):
        near = [cells(xl_ref, 0, t), cells(xl_ref, 1, t)] + [cells(w_ref, x, t) for x in range(3)]
        a, b = outer_faces(near, 0)
        put(xc, 0, t, minus(a, b))
        put(xc, 1, t, b)
        far = [cells(w_ref, x, t) for x in range(13, 16)] + [cells(xh_ref, 0, t), cells(xh_ref, 1, t)]
        a, b = outer_faces(far, 0)
        put(xc, 2, t, [-v for v in a])
        put(xc, 3, t, minus(a, b))
        return 0

    lax.fori_loop(0, TS, column, 0, unroll=4)
    rows = w_ref.reshape(XS * 256, 128)
    packed = yc.reshape(XS * 128, 128)
    zero = jnp.zeros((8, 128), jnp.float32)

    def clear(x, _):
        for part in range(2):
            for k in range(FIELDS):
                yc[x, part, k] = zero
        return 0

    lax.fori_loop(0, XS, clear, 0, unroll=4)

    def store(half, part, y, values):
        for k in range(FIELDS):
            packed[pl.ds(half * 1024 + part * 64 + k * 8 + y, 8, stride=128), :] = values[k]

    for half in range(2):
        own = lambda y: [y_layer(rows, half, k, y) for k in range(FIELDS)]
        sent = lambda layer, near: [jnp.where(near, yn_ref[layer, half, k], yf_ref[layer, half, k]) for k in range(FIELDS)]
        a, b = outer_faces([sent(0, core == 1), sent(1, core == 1), own(0), own(1), own(2)], 1)
        store(half, 0, 0, minus(a, b))
        store(half, 0, 1, b)
        a, b = outer_faces([own(29), own(30), own(31), sent(0, core == 0), sent(1, core == 0)], 1)
        store(half, 1, 6, [-v for v in a])
        store(half, 1, 7, minus(a, b))


def changes(inner, xc, yc, x, t, edge):
    xz_ref, y_ref = inner
    total = plus(cells(xz_ref, x, t), cells(y_ref, x, t))
    if t in (0, 3):
        total = plus(total, cells(yc, x, t // 3))
    if edge is not None:
        total = plus(total, cells(xc, edge, t))
    return total


def each_layer(work):
    for edge, x in enumerate((0, 1, XS - 2, XS - 1)):
        work(x, edge)
    lax.fori_loop(2, XS - 2, lambda x, _: (work(x, None), 0)[1], 0, unroll=12)


def step_of(tile_ref):
    return COURANT / jnp.broadcast_to(tile_ref[1:2, :], (8, 128))


def first_kernel(place_ref, tile_ref, w_ref, u_ref, txz, ty, xl, xh, yn, yf, s_ref, w2_ref, xl_ref, xh_ref, yn_ref, yf_ref, xc, yc):
    step = step_of(tile_ref)
    core = place_ref[0] % 2
    outer(core, w_ref, (xl, xh, yn, yf), xc, yc)

    def work(x, edge):
        for t in range(TS):
            change = changes((txz, ty), xc, yc, x, t, edge)
            state = cells(u_ref, x, t)
            first = [u + step * c for u, c in zip(state, change)]
            put(s_ref, x, t, [0.5 * (u + f) for u, f in zip(state, first)])
            put(w2_ref, x, t, primitive(first))

    each_layer(work)
    pack_sides(core, w2_ref, xl_ref, xh_ref, yn_ref, yf_ref)


def second_kernel(place_ref, tile_ref, w_ref, s_ref, txz, ty, xl, xh, yn, yf, out_ref, xc, yc, blocks, sems):
    step = 0.5 * step_of(tile_ref)
    outer(place_ref[0] % 2, w_ref, (xl, xh, yn, yf), xc, yc)
    index, flip = swap_indices()
    rows = blocks.reshape(BLK_DEV * CHUNKS * FIELDS, 128)

    def work(x, edge):
        for t in range(TS):
            change = changes((txz, ty), xc, yc, x, t, edge)
            chunk = 2 * x + t % 2
            for k, (s, c) in enumerate(zip(cells(s_ref, x, t), change)):
                start = ((t // 2) * 8 * CHUNKS + chunk) * 8 + k
                rows[pl.ds(start, 8, stride=CHUNKS * 8), :] = swapped(s + step * c, index, flip)

    def part(quarter):
        chunks = pl.ds(quarter * 8, 8)
        return pltpu.make_async_copy(blocks.at[:, chunks], out_ref.at[:, chunks], sems.at[quarter])

    def pairs(first, last):
        lax.fori_loop(first, last, lambda x, _: (work(x, None), 0)[1], 0, unroll=last - first)

    work(0, 0)
    work(1, 1)
    pairs(2, 8)
    part(0).start()
    part(1).start()
    pairs(8, 12)
    part(2).start()
    pairs(12, 14)
    work(14, 2)
    work(15, 3)
    part(3).start()
    for quarter in range(4):
        part(quarter).wait()


VMEM = pl.BlockSpec(memory_space=pltpu.VMEM)
SMEM = pl.BlockSpec(memory_space=pltpu.SMEM)
ANY = pl.BlockSpec(memory_space=pl.ANY)
HBM = pl.BlockSpec(memory_space=pltpu.HBM)


def shape(dims):
    return pltpu.VMEM(dims, jnp.float32)


def kernel(function, in_specs, outs, scratch, name, flops, limit=LIMIT, out_spec=VMEM):
    single = not isinstance(outs, list)
    return pl.pallas_call(
        function,
        out_shape=jax.ShapeDtypeStruct(outs, jnp.float32) if out_spec is ANY else shape(outs) if single else [shape(dims) for dims in outs],
        in_specs=in_specs,
        out_specs=out_spec if single else [out_spec] * len(outs),
        scratch_shapes=scratch,
        name=name,
        compiler_params=pltpu.CompilerParams(vmem_limit_bytes=limit),
        cost_estimate=pl.CostEstimate(flops=flops, bytes_accessed=6 << 20, transcendentals=0),
    )


def shifted(value, axis, by):
    count = lax.axis_size(axis)
    return lax.ppermute(value, axis, [(i, (i + by) % count) for i in range(count)])


def exchanged(xl, xh, yn, yf):
    count = lax.axis_size("dev")
    near = [(i, i ^ 1) for i in range(count)]
    far = [(i, (i + 1) % count if i % 2 else (i - 1) % count) for i in range(count)]
    return shifted(xh, "group", 1), shifted(xl, "group", -1), lax.ppermute(yn, "dev", near), lax.ppermute(yf, "dev", far)


def body(blocks_in, counts):
    devices = lax.axis_size(AXES)
    place = lax.axis_index(AXES).astype(jnp.int32).reshape(1)
    tiles = lambda value: value.reshape(value.shape[0], FIELDS, CHUNKS, 128).swapaxes(1, 2)
    own = tiles(blocks_in)
    passed = (BLK_DEV - 1, CHUNKS, FIELDS, 128)
    there = pltpu.with_memory_space_constraint(own, pltpu.HBM)
    outgoing = kernel(outgoing_kernel, [SMEM, HBM], passed, [pltpu.SemaphoreType.DMA((BLK_DEV - 1,))], "outgoing", 1 << 10)(
        counts, there
    )
    came = lax.ppermute(outgoing, AXES, [(i, i + 1) for i in range(devices - 1)])
    tile = kernel(
        speed_kernel,
        [SMEM, SMEM, HBM],
        (8, 128),
        [
            pltpu.VMEM((blocks_in.shape[0], CHUNKS, FIELDS, 128), jnp.float32),
            pltpu.SemaphoreType.DMA((pl.cdiv(blocks_in.shape[0], 4),)),
        ],
        "signal_speed",
        1 << 20,
    )(counts, place, there)
    tile = jnp.maximum(tile, lax.ppermute(tile, AXES, [(i, i ^ 1) for i in range(devices)]))
    for masks in ROUNDS:
        tile = jnp.maximum(tile, lax.ppermute(tile, AXES, [(i, i ^ masks[i % 2]) for i in range(devices)]))
    tile = jnp.maximum(tile, lax.ppermute(tile, AXES, [(i, i ^ 1) for i in range(devices)]))
    sides = [XFACE, XFACE, YFACE, YFACE]
    u, w, *faces = kernel(
        assemble_kernel,
        [SMEM, VMEM, ANY, ANY],
        [GRID, GRID] + sides,
        [pltpu.VMEM((2, CHUNKS, 8, FIELDS, 128), jnp.float32), pltpu.SemaphoreType.DMA((BLK_DEV,))],
        "assemble",
        1 << 20,
    )(place, tile, pltpu.with_memory_space_constraint(came, pltpu.HBM), there)
    corrections = [pltpu.VMEM((4, TS, FIELDS, 8, 128), jnp.float32), pltpu.VMEM((XS, 2, FIELDS, 8, 128), jnp.float32)]
    inner = kernel(inner_kernel, [VMEM], [GRID] * 2, [pltpu.VMEM(GRID, jnp.float32)] * 4, "inner_fluxes", 40 << 20)
    specs = [SMEM] + [VMEM] * 9
    ghosts = exchanged(*faces)
    s, w2, *faces = kernel(first_kernel, specs, [GRID, GRID] + sides, corrections, "first_stage", 1 << 20)(
        place, tile, w, u, *inner(w), *ghosts
    )
    ghosts = exchanged(*faces)
    result = (BLK_DEV, CHUNKS, FIELDS, 128)
    buffers = corrections + [pltpu.VMEM(result, jnp.float32), pltpu.SemaphoreType.DMA((4,))]
    out = kernel(second_kernel, specs, result, buffers, "second_stage", 1 << 20, out_spec=ANY)(
        place, tile, w2, s, *inner(w2), *ghosts
    )
    return out.swapaxes(1, 2).reshape(BLK_DEV, FIELDS, BS * BS * BS)


def solution(mesh):
    in_specs = (P(AXES, None, None), P(AXES))
    out_specs = P(AXES, None, None)
    return jax.shard_map(body, mesh=mesh, in_specs=in_specs, out_specs=out_specs, check_vma=False)
```
